32 devices in a mesh: blk: 8 (over z, x), narrow: 4 (over y, core).
Axes of the slice: x: 2, y: 2, z: 4, core: 2. Of those that a mesh axis runs over, the one named last changes fastest.
Arguments:
- query_ids: int32 [2, 32, 32], P(None, ('blk', 'narrow')), may hold values from 0 to 30719, as said below
- passage_ids: int32 [2, 32, 512], P(None, ('blk', 'narrow')), may hold values from 0 to 30719, as said below
- passage_len: int32 [2, 32], P(None, ('blk', 'narrow')), may hold values from 1 to 512, 8192 in all within a row
- positives: int32 [2, 4, 8], P(None, 'narrow'), may hold values from 0 to 7
- domains: int32 [2, 4, 8], P(None, 'narrow'), may hold values from 0 to 3
- table: float32 [30720, 768], P(('blk', 'narrow')), may hold values from -0.3125 to 0.3125
- table_m: float32 [30720, 768], P(('blk', 'narrow')), may hold values from -5.722046e-06 to 5.722046e-06
- table_v: float32 [30720, 768], P(('blk', 'narrow')), may hold values from 4.1702596e-12 to 1.6681038e-11
- pos_table: float32 [512, 768], P(None, 'narrow'), may hold values from -0.3125 to 0.3125
- pos_m: float32 [512, 768], P(None, 'narrow'), may hold values from -5.722046e-06 to 5.722046e-06
- pos_v: float32 [512, 768], P(None, 'narrow'), may hold values from 4.1702596e-12 to 1.6681038e-11
- vector: float32 [1, 10752], P(None, 'narrow')
- vector_m: float32 [1, 10752], P(None, 'narrow'), may hold values from -2.2888184e-05 to 2.2888184e-05
- vector_v: float32 [1, 10752], P(None, 'narrow'), may hold values from 6.736573e-11 to 2.6946292e-10
- w_qkv: float32 [768, 2304], P(None, 'narrow'), may hold values from -0.21875 to 0.21875
- m_qkv: float32 [768, 2304], P(None, 'narrow'), may hold values from -5.340576e-05 to 5.340576e-05
- w_attn: float32 [768, 768], P(None, 'narrow'), may hold values from -3.5 to 3.5
- m_attn: float32 [768, 768], P(None, 'narrow'), may hold values from -5.340576e-05 to 5.340576e-05
- w_in: float32 [768, 3072], P(None, 'narrow'), may hold values from -0.21875 to 0.21875
- m_in: float32 [768, 3072], P(None, 'narrow'), may hold values from -5.340576e-05 to 5.340576e-05
- w_out: float32 [768, 3072], P(None, 'narrow'), may hold values from -0.109375 to 0.109375
- m_out: float32 [768, 3072], P(None, 'narrow'), may hold values from -5.340576e-05 to 5.340576e-05
- w_proj: float32 [128, 768], P(None, 'narrow'), may hold values from -0.21875 to 0.21875
- m_proj: float32 [128, 768], P(None, 'narrow'), may hold values from -5.340576e-05 to 5.340576e-05
Outputs:
- loss: float32 [], replicated
- grad_norm: float32 [], replicated
- table_new: float32 [30720, 768], P(('blk', 'narrow'))
- table_m_new: float32 [30720, 768], P(('blk', 'narrow'))
- table_v_new: float32 [30720, 768], P(('blk', 'narrow'))
- pos_new: float32 [512, 768], P(None, 'narrow')
- pos_m_new: float32 [512, 768], P(None, 'narrow')
- pos_v_new: float32 [512, 768], P(None, 'narrow')
- vector_new: float32 [1, 10752], P(None, 'narrow')
- vector_m_new: float32 [1, 10752], P(None, 'narrow')
- vector_v_new: float32 [1, 10752], P(None, 'narrow')
- qkv_new: float32 [768, 2304], P(None, 'narrow')
- qkv_mom: float32 [768, 2304], P(None, 'narrow')
- attn_new: float32 [768, 768], P(None, 'narrow')
- attn_mom: float32 [768, 768], P(None, 'narrow')
- in_new: float32 [768, 3072], P(None, 'narrow')
- in_mom: float32 [768, 3072], P(None, 'narrow')
- out_new: float32 [768, 3072], P(None, 'narrow')
- out_mom: float32 [768, 3072], P(None, 'narrow')
- proj_new: float32 [128, 768], P(None, 'narrow')
- proj_mom: float32 [128, 768], P(None, 'narrow')
- attn_bias_grad: float32 [1, 768], P(None, 'narrow')
The draws below stay inside these ranges and needn't reach their ends.
Inputs may be any that keep to these rules, and one draw needn't show every extreme that they name: `query_ids`: counting all token slots of one device together (its query and passage of every micro-batch, unused slots too), at most 36 have ids in any one block of 960 consecutive ids starting at a multiple of 960, and exactly 36 in some block. `passage_ids`: the same bound of 36 holds for these slots together with the query slots of the same device. `passage_len`: in each micro-batch the longest passage has exactly 512 tokens.
All inputs are finite; a program needn't handle non-finite values. No bound on the sum of `passage_len` on one device may be relied on, other than what follows from the above.
Results may differ from the reference program's by a relative error of at most 0.015.
Values may be sent and summed in bfloat16 or wider, within the bound.
No kernel may reach another device: no remote copies, remote signals or barrier semaphores. Data moves between devices by JAX's collectives and lax.ppermute only.
A program may use at most 384 MiB of HBM per device.

```python
import math
import jax
import jax.numpy as jnp
import numpy as np
from jax import lax

D = 768
HEADS = 12
HDIM = 64
FF = 3072
VOCAB = 30720
VDIM = 128
QLEN = 32
PLEN = 512
MICRO = 2
DOMAINS = 4
STEP = 10
QUERIES = 32
CAP = 36
NV = 10752
N_BLK = 8
N_NARROW = 4


def token_grid(key):
    slots = MICRO * (QLEN + PLEN)
    owners = QUERIES
    shard = VOCAB // QUERIES
    limit = CAP

    def one_device(device_key):
        keys = jax.random.split(device_key, 4)
        full = jax.random.randint(keys[0], (), 0, owners)
        others = jax.random.permutation(keys[1], (owners - 1) * limit)[:slots - limit] // limit
        others = jnp.where(others >= full, others + 1, others)
        chosen = jnp.concatenate([jnp.zeros((limit,), jnp.int32) + full, others.astype(jnp.int32)])
        chosen = chosen[jax.random.permutation(keys[2], slots)]
        offsets = jax.random.randint(keys[3], (slots,), 0, shard)
        return (chosen * shard + offsets).astype(jnp.int32)
    grid = jax.vmap(one_device)(jax.random.split(key, owners))
    return grid.reshape(owners, MICRO, QLEN + PLEN).transpose(1, 0, 2)


def draw_query_ids(key, part):
    return token_grid(key)[:, :, :QLEN]


def draw_passage_ids(key, part):
    return token_grid(key)[:, :, QLEN:]


def draw_vector(key, part):
    key = jax.random.fold_in(key, 7)
    spots = jnp.arange(10 * D + FF)
    gains = (spots < D) | (spots >= 5 * D) & (spots < 6 * D) | (spots >= 8 * D + FF) & (spots < 9 * D + FF)
    noise = jax.random.normal(key, (1, 10 * D + FF), jnp.float32)
    return jnp.where(gains[None, :], 1.0 + 0.1 * noise, 0.2 * noise)


def plant(entries, stream_key, least, largest):
    spot = [jax.random.randint(jax.random.fold_in(stream_key, axis), (), 0, length) for axis, length in enumerate(entries.shape)]
    widest = entries.shape.index(max(entries.shape))
    next_to = spot[:widest] + [(spot[widest] + 1) % entries.shape[widest]] + spot[widest + 1:]
    return entries.at[tuple(spot)].set(least).at[tuple(next_to)].set(largest)


def steps_of(key, shape, cuts, low, high):
    factor_of = 1.0
    for axis_at, parts in cuts:
        heights = jax.random.uniform(jax.random.fold_in(jax.random.fold_in(key, 6), axis_at), (parts,), jnp.float32, low / len(cuts), high / len(cuts))
        factor_of = factor_of * jnp.repeat(jnp.exp(heights), shape[axis_at] // parts).reshape((-1,) + (1,) * (len(shape) - 1 - axis_at))
    return factor_of


def profile(amount, total, most, skew):
    weights = [(1 << 20) // math.isqrt(rank ** skew) + 1 for rank in range(2, amount + 1)]
    surplus, counts = total - most - (amount - 1), [1] * (amount - 1)
    while surplus > 0:
        free = [i for i in range(amount - 1) if counts[i] < most]
        pool, left = sum([weights[i] for i in free]), surplus
        for i in free:
            more = min(most - counts[i], max(1, left * weights[i] // pool), surplus)
            counts[i] = counts[i] + more
            surplus = surplus - more
    return np.array([most] + counts)


def ragged_sizes(key, number_of, total, most, skew):
    if number_of == 2:
        one = jax.random.randint(key, (), max(1, total - most), min(most, total - 1) + 1)
        return jnp.stack([one, total - one])
    sizes = jnp.asarray(profile(number_of, total, most, skew), jnp.int32)
    twos = (number_of - 1) // 2
    source_of, taker = sizes[1:1 + 2 * twos:2], sizes[2:2 + 2 * twos:2]
    margin = jnp.minimum(source_of - 1, most - taker)
    passed = jax.random.randint(jax.random.fold_in(key, 1), (twos,), 0, 1 << 20) % (margin + 1)
    sizes = sizes.at[1:1 + 2 * twos:2].set(source_of - passed).at[2:2 + 2 * twos:2].set(taker + passed)
    return sizes[jax.random.permutation(jax.random.fold_in(key, 2), number_of)]


def normal_values(rng, shape, scale, most, cuts=(), kind=jnp.bfloat16):
    gain = steps_of(rng, shape, cuts, -0.22, 0.18) if cuts else 1.0
    values = jax.random.normal(rng, shape, jnp.float32) * scale * gain
    return jnp.minimum(jnp.maximum(values, -most), most).astype(kind)


def setup_inputs(seed: int = 0) -> dict:
    key_of = jax.random.split(jax.random.key(seed), 25)
    query_ids = draw_query_ids(jax.random.fold_in(key_of[24], 71), 0)
    passage_ids = draw_passage_ids(jax.random.fold_in(key_of[24], 71), 0)
    passage_len = jax.vmap(lambda own: ragged_sizes(own, QUERIES, QUERIES * PLEN // 2, PLEN, 2))(jax.random.split(key_of[2], MICRO)).reshape((MICRO, QUERIES)).astype(jnp.int32)
    positives = plant(jax.random.randint(key_of[3], (MICRO, N_NARROW, N_BLK), 0, N_BLK), jax.random.fold_in(key_of[3], 1), 0, N_BLK - 1).astype(jnp.int32)
    domains = plant(jax.random.randint(key_of[4], (MICRO, N_NARROW, N_BLK), 0, DOMAINS), jax.random.fold_in(key_of[4], 1), 0, DOMAINS - 1).astype(jnp.int32)
    table = normal_values(key_of[5], (VOCAB, D), 0.05, 0.3125, ((0, 32),), jnp.float32)
    table_m = normal_values(key_of[6], (VOCAB, D), (0.0055 * (VOCAB * D + PLEN * D + 4 * D * D + 2 * D * FF + VDIM * D + NV) ** -0.5), 5.7220458984375e-06, ((0, 32),), jnp.float32)
    table_v = jnp.clip(jnp.exp(math.log(1.6681038494947842e-11) - 1.3862944 * jax.random.uniform(key_of[7], (VOCAB, D), jnp.float32) ** steps_of(key_of[7], (VOCAB, D), ((0, 32),), -0.2, 0.2)), 4.1702596237369605e-12, 1.6681038494947842e-11)
    pos_table = normal_values(key_of[8], (PLEN, D), 0.05, 0.3125, ((1, 4),), jnp.float32)
    pos_m = normal_values(key_of[9], (PLEN, D), (0.0055 * (VOCAB * D + PLEN * D + 4 * D * D + 2 * D * FF + VDIM * D + NV) ** -0.5), 5.7220458984375e-06, ((1, 4),), jnp.float32)
    pos_v = jnp.clip(jnp.exp(math.log(1.6681038494947842e-11) - 1.3862944 * jax.random.uniform(key_of[10], (PLEN, D), jnp.float32) ** steps_of(key_of[10], (PLEN, D), ((1, 4),), -0.2, 0.2)), 4.1702596237369605e-12, 1.6681038494947842e-11)
    vector = draw_vector(jax.random.fold_in(key_of[24], 71), 0)
    vector_m = normal_values(key_of[12], (1, NV), (0.022 * (VOCAB * D + PLEN * D + 4 * D * D + 2 * D * FF + VDIM * D + NV) ** -0.5), 2.288818359375e-05, ((1, 4),), jnp.float32)
    vector_v = jnp.clip(jnp.exp(math.log(2.6946292419616213e-10) - 1.3862944 * jax.random.uniform(key_of[13], (1, NV), jnp.float32) ** steps_of(key_of[13], (1, NV), ((1, 4),), -0.2, 0.2)), 6.736573104904053e-11, 2.6946292419616213e-10)
    w_qkv = normal_values(key_of[14], (D, 3 * D), D ** -0.5, 0.21875, ((1, 4),), jnp.float32)
    m_qkv = normal_values(key_of[15], (D, 3 * D), (0.05 * (VOCAB * D + PLEN * D + 4 * D * D + 2 * D * FF + VDIM * D + NV) ** -0.5), 5.340576171875e-05, ((1, 4),), jnp.float32)
    w_attn = normal_values(key_of[16], (D, D), (max(2 * D // PLEN, 1)) ** -0.5, 3.5, ((1, 4),), jnp.float32)
    m_attn = normal_values(key_of[17], (D, D), (0.05 * (VOCAB * D + PLEN * D + 4 * D * D + 2 * D * FF + VDIM * D + NV) ** -0.5), 5.340576171875e-05, ((1, 4),), jnp.float32)
    w_in = normal_values(key_of[18], (D, FF), D ** -0.5, 0.21875, ((1, 4),), jnp.float32)
    m_in = normal_values(key_of[19], (D, FF), (0.05 * (VOCAB * D + PLEN * D + 4 * D * D + 2 * D * FF + VDIM * D + NV) ** -0.5), 5.340576171875e-05, ((1, 4),), jnp.float32)
    w_out = normal_values(key_of[20], (D, FF), FF ** -0.5, 0.109375, ((1, 4),), jnp.float32)
    m_out = normal_values(key_of[21], (D, FF), (0.05 * (VOCAB * D + PLEN * D + 4 * D * D + 2 * D * FF + VDIM * D + NV) ** -0.5), 5.340576171875e-05, ((1, 4),), jnp.float32)
    w_proj = normal_values(key_of[22], (VDIM, D), D ** -0.5, 0.21875, ((1, 4),), jnp.float32)
    m_proj = normal_values(key_of[23], (VDIM, D), (0.05 * (VOCAB * D + PLEN * D + 4 * D * D + 2 * D * FF + VDIM * D + NV) ** -0.5), 5.340576171875e-05, ((1, 4),), jnp.float32)
    return {"query_ids": query_ids, "passage_ids": passage_ids, "passage_len": passage_len, "positives": positives, "domains": domains, "table": table, "table_m": table_m, "table_v": table_v, "pos_table": pos_table, "pos_m": pos_m, "pos_v": pos_v, "vector": vector, "vector_m": vector_m, "vector_v": vector_v, "w_qkv": w_qkv, "m_qkv": m_qkv, "w_attn": w_attn, "m_attn": m_attn, "w_in": w_in, "m_in": m_in, "w_out": w_out, "m_out": m_out, "w_proj": w_proj, "m_proj": m_proj}


@jax.custom_vjp
def low(v):
    return lax.optimization_barrier(v.astype(jnp.bfloat16)).astype(jnp.float32)

@jax.custom_vjp
def low_back(v):
    return v

def low_keep(v):
    return (low(v), None)

def low_pass(kept, grad):
    return (grad,)

def back_keep(v):
    return (v, None)

def back_low(kept, grad):
    return (low(grad),)
low.defvjp(low_keep, low_pass)
low_back.defvjp(back_keep, back_low)
highest = lax.Precision.HIGHEST
norm_eps = 1e-12
smoothing = 0.1
masked = -1e+30
newton_one = 3.4445
newton_two = -4.775
newton_three = 2.0315
muon_rate = 0.1
attn_rate = 1.0
muon_moment = 0.95
weight_decay = 0.01
adam_rate = 0.02
vector_rate = 0.25
beta_one = 0.9
beta_two = 0.95
adam_eps = 1e-08
clip_limit = 0.05

def product(operand, other):
    return jnp.dot(operand, other, precision=highest, preferred_element_type=jnp.float32)

def rounded(values):
    return low(low_back(values))

def layer_norm(values, norm_gain, norm_shift):
    centred = values - lax.optimization_barrier(jnp.mean(values, axis=-1, keepdims=True))
    spread = lax.optimization_barrier(jnp.mean(centred * centred, axis=-1, keepdims=True))
    return centred * lax.rsqrt(spread + norm_eps) * norm_gain + norm_shift

def encode(token_rows, positions, weights, vector, usable):
    w_qkv, w_attn, w_in, w_out, w_proj = weights
    length = token_rows.shape[0]
    bounds = [0, D, 2 * D, 3 * D, 4 * D, 5 * D, 6 * D, 7 * D, 7 * D + FF, 8 * D + FF, 9 * D + FF, 10 * D + FF]
    pieces = [vector[bounds[index]:bounds[index + 1]] for index in range(11)]
    normed = layer_norm(token_rows + positions, pieces[0], pieces[1])
    offset_qkv = jnp.concatenate([pieces[2], jnp.zeros_like(pieces[2]), pieces[3]])
    qkv_rows = rounded(product(rounded(normed), w_qkv) + offset_qkv).reshape(length, 3, HEADS, HDIM)
    scores = low_back(jnp.einsum('qhd,khd->hqk', qkv_rows[:, 0], qkv_rows[:, 1], precision=highest) * HDIM ** (-0.5))
    scores = jnp.where(usable[None, None, :], scores, masked)
    exponent = jnp.exp(scores - lax.optimization_barrier(jnp.max(scores, axis=-1, keepdims=True)))
    attend = exponent / lax.optimization_barrier(jnp.sum(exponent, axis=-1, keepdims=True))
    context = jnp.einsum('hqk,khd->qhd', low(attend), qkv_rows[:, 2], precision=highest).reshape(length, D)
    hidden = layer_norm(normed + low_back(product(rounded(context), w_attn)) + pieces[4], pieces[5], pieces[6])
    widened = jax.nn.gelu(low_back(product(rounded(hidden), w_in)) + pieces[7], approximate=False)
    output_rows = layer_norm(hidden + low_back(product(rounded(widened), w_out.T)) + pieces[8], pieces[9], pieces[10])
    embedded = low_back(product(rounded(output_rows), w_proj.T))
    return rounded(embedded * lax.rsqrt(lax.optimization_barrier(jnp.sum(embedded * embedded, axis=-1, keepdims=True)) + 1e-06))

def score_group(query_group, passage_vectors, usable):
    sims = low_back(jnp.einsum('bik,jk->bij', query_group, passage_vectors, precision=highest))
    scaled = jnp.where(usable[None, None, :], sims / smoothing, masked)
    summit = lax.optimization_barrier(jnp.max(scaled, axis=-1, keepdims=True))
    smooth = smoothing * (summit[..., 0] + jnp.log(lax.optimization_barrier(jnp.sum(jnp.exp(scaled - summit), axis=-1))))
    return lax.optimization_barrier(jnp.sum(smooth, axis=-1))

def total_loss(params, query_ids, passage_ids, passage_len, positives, domains):
    table, pos_table, vector, weights = params
    low_table = low(table)
    low_pos = low(pos_table)
    low_vector = low(vector)[0]
    low_weights = tuple((low(member) for member in weights))
    positions = jnp.arange(PLEN)
    loss_sum = jnp.zeros((), jnp.float32)
    for micro in range(MICRO):

        def query_side(ids_row):
            return encode(low_table[ids_row], low_pos[:QLEN], low_weights, low_vector, jnp.ones((QLEN,), jnp.bool_))

        def passage_side(paired):
            return encode(low_table[paired[0]], low_pos, low_weights, low_vector, positions < paired[1])
        query_vecs = lax.map(jax.checkpoint(query_side), query_ids[micro])
        passage_vecs = lax.map(jax.checkpoint(passage_side), (passage_ids[micro], passage_len[micro]))
        grouped = query_vecs.reshape(N_BLK, N_NARROW, QLEN, VDIM)

        def passage_scores(paired):
            vectors, length, number = paired
            return score_group(jnp.take(grouped, number % N_NARROW, axis=1), vectors, positions < length)
        scores = lax.map(jax.checkpoint(passage_scores), (passage_vecs, passage_len[micro], jnp.arange(N_BLK * N_NARROW)))
        scores = scores.reshape(N_BLK, N_NARROW, N_BLK)
        labels = domains[micro]
        query_labels = jnp.take_along_axis(labels, positives[micro], axis=1)
        allowed = labels.T[:, :, None] == query_labels[None]
        summit = lax.optimization_barrier(jnp.max(jnp.where(allowed, scores, masked), axis=0))
        mass = lax.optimization_barrier(jnp.sum(jnp.where(allowed, jnp.exp(scores - summit[None]), 0.0), axis=0))
        log_total = summit + jnp.log(mass)
        matched = jnp.take_along_axis(scores.transpose(1, 2, 0), positives[micro][..., None], axis=2)[..., 0]
        loss_sum = loss_sum + jnp.sum(log_total - matched)
    return loss_sum

def adam_step(weight, first, second, gradient, rate):
    first_new = beta_one * first + (1.0 - beta_one) * gradient
    second_new = beta_two * second + (1.0 - beta_two) * gradient * gradient
    update = first_new / (1.0 - beta_one ** STEP) / (jnp.sqrt(second_new / (1.0 - beta_two ** STEP)) + adam_eps)
    return (weight - rate * (update + weight_decay * weight), first_new, second_new)

def muon_step(weight, moment, gradient, rate):
    renewed = muon_moment * moment + gradient
    ortho = renewed / (jnp.sqrt(jnp.sum(renewed * renewed)) + 1e-07)
    for iteration in range(5):
        gram = product(ortho, ortho.T)
        ortho = newton_one * ortho + product(newton_two * gram + newton_three * product(gram, gram), ortho)
    scale = 0.2 * max(weight.shape) ** 0.5
    return (weight - rate * (scale * ortho + weight_decay * weight), renewed)

def reference(query_ids, passage_ids, passage_len, positives, domains, table, table_m, table_v, pos_table, pos_m, pos_v, vector, vector_m, vector_v, w_qkv, m_qkv, w_attn, m_attn, w_in, m_in, w_out, m_out, w_proj, m_proj):
    params = (table, pos_table, vector, (w_qkv, w_attn, w_in, w_out, w_proj))

    def objective(values):
        return total_loss(values, query_ids, passage_ids, passage_len, positives, domains)
    loss, pullback = jax.vjp(objective, params)
    grads, = pullback(jnp.ones((), jnp.float32))
    flat = [grads[0], grads[1], grads[2]] + list(grads[3])
    grad_norm = jnp.sqrt(sum((jnp.sum(member * member) for member in flat)))
    factor = jnp.minimum(1.0, clip_limit / (grad_norm + 1e-06))
    attn_bias_grad = factor * grads[2][:, 4 * D:5 * D]
    table_new, table_m_new, table_v_new = adam_step(table, table_m, table_v, factor * grads[0], adam_rate)
    pos_new, pos_m_new, pos_v_new = adam_step(pos_table, pos_m, pos_v, factor * grads[1], adam_rate)
    vector_new, vector_m_new, vector_v_new = adam_step(vector, vector_m, vector_v, factor * grads[2], vector_rate)
    qkv_new, qkv_mom = muon_step(w_qkv, m_qkv, factor * grads[3][0], muon_rate)
    attn_new, attn_mom = muon_step(w_attn, m_attn, factor * grads[3][1], attn_rate)
    in_new, in_mom = muon_step(w_in, m_in, factor * grads[3][2], muon_rate)
    out_new, out_mom = muon_step(w_out, m_out, factor * grads[3][3], muon_rate)
    proj_new, proj_mom = muon_step(w_proj, m_proj, factor * grads[3][4], muon_rate)
    return (loss, grad_norm, table_new, table_m_new, table_v_new, pos_new, pos_m_new, pos_v_new, vector_new, vector_m_new, vector_v_new, qkv_new, qkv_mom, attn_new, attn_mom, in_new, in_mom, out_new, out_mom, proj_new, proj_mom, attn_bias_grad)
```

```python
import functools

import jax
import jax.numpy as jnp
from jax import lax
from jax.experimental import pallas as pl
from jax.experimental.pallas import tpu as pltpu
from jax.sharding import PartitionSpec as P

D = 768
HEADS = 12
HDIM = 64
FF = 3072
VDIM = 128
STEP = 10
MATRICES = 4

norm_eps = 1e-12
smoothing = 0.1
masked = -1e30
newton_one = 3.4445
newton_two = -4.775
newton_three = 2.0315
muon_rate = 0.1
attn_rate = 1.0
muon_moment = 0.95
weight_decay = 0.01
adam_rate = 0.02
vector_rate = 0.25
beta_one = 0.9
beta_two = 0.95
adam_eps = 1e-08
clip_limit = 0.05

bf16 = jnp.bfloat16
f32 = jnp.float32
SLOT_CAPS = {960: 36, 120: 7}


def round_up(value, step):
    return -(-value // step) * step


def dot_nn(left, right):
    return lax.dot_general(left, right, (((1,), (0,)), ((), ())), preferred_element_type=f32)


def dot_nt(left, right):
    return lax.dot_general(left, right, (((1,), (1,)), ((), ())), preferred_element_type=f32)


def dot_tn(left, right):
    return lax.dot_general(left, right, (((0,), (0,)), ((), ())), preferred_element_type=f32)


def low(values):
    return values.astype(bf16)


def norm_forward(values, gain, shift):
    centred = values - jnp.mean(values, axis=-1, keepdims=True)
    spread = jnp.mean(centred * centred, axis=-1, keepdims=True)
    scale = lax.rsqrt(spread + norm_eps)
    hat = centred * scale
    return hat * gain + shift, hat, scale


def norm_backward(grad, hat, scale, gain):
    d_hat = grad * gain
    first = jnp.mean(d_hat, axis=-1, keepdims=True)
    second = jnp.mean(d_hat * hat, axis=-1, keepdims=True)
    return scale * (d_hat - first - hat * second)


def gelu_parts(values):
    cdf = 0.5 * (1.0 + lax.erf(values * (0.5**0.5)))
    density = jnp.exp(-0.5 * values * values) * 0.3989422804014327
    return values * cdf, cdf + values * density


def attention_forward_kernel(lens_ref, qkv_ref, out_ref, *, query_len, span):
    used = lens_ref[pl.program_id(0)]
    bias_long = jnp.where(lax.broadcasted_iota(jnp.int32, (1, span), 1) < used, 0.0, masked)

    def attend(first, count, lane, half, bias):
        rows = pl.ds(first, count)
        queries = qkv_ref[rows, pl.ds(lane, 128)][:, half]
        keys = qkv_ref[rows, pl.ds(lane + D, 128)][:, half]
        values = qkv_ref[rows, pl.ds(lane + 2 * D, 128)][:, half]
        scores = dot_nt(queries * bf16(HDIM**-0.5), keys)
        if bias is not None:
            scores = scores + bias
        exponent = jnp.exp(scores - jnp.max(scores, axis=-1, keepdims=True))
        attend_low = low(exponent * (1.0 / jnp.sum(exponent, axis=-1, keepdims=True)))
        return dot_nn(attend_low, values)

    def pair(index, carry):
        lane = pl.multiple_of(index * 128, 128)
        halves = (slice(0, HDIM), slice(HDIM, 128))
        for first, count, bias in ((0, query_len, None), (query_len, span, bias_long)):
            both = [attend(first, count, lane, half, bias) for half in halves]
            out_ref[pl.ds(first, count), pl.ds(lane, 128)] = low(jnp.concatenate(both, axis=1))
        return carry

    lax.fori_loop(0, HEADS // 2, pair, 0)


def attention_backward_kernel(lens_ref, qkv_ref, grad_ref, out_ref, *, query_len, span):
    used = lens_ref[pl.program_id(0)]
    bias_long = jnp.where(lax.broadcasted_iota(jnp.int32, (span, 1), 0) < used, 0.0, masked)

    def attend(first, count, lane, half, bias):
        rows = pl.ds(first, count)
        queries = qkv_ref[rows, pl.ds(lane, 128)][:, half] * bf16(HDIM**-0.5)
        keys = qkv_ref[rows, pl.ds(lane + D, 128)][:, half]
        values = qkv_ref[rows, pl.ds(lane + 2 * D, 128)][:, half]
        grads = grad_ref[rows, pl.ds(lane, 128)][:, half]
        scores = dot_nt(keys, queries)
        if bias is not None:
            scores = scores + bias
        exponent = jnp.exp(scores - jnp.max(scores, axis=0, keepdims=True))
        share = exponent * (1.0 / jnp.sum(exponent, axis=0, keepdims=True))
        d_share = dot_nt(values, grads)
        d_values = dot_nn(low(share), grads)
        weighted = share * d_share
        d_scores = low(weighted - share * jnp.sum(weighted, axis=0, keepdims=True))
        d_keys = dot_nn(d_scores, queries)
        d_queries = dot_tn(d_scores, keys) * HDIM**-0.5
        return d_queries, d_keys, d_values

    def pair(index, carry):
        lane = pl.multiple_of(index * 128, 128)
        halves = (slice(0, HDIM), slice(HDIM, 128))
        for first, count, bias in ((0, query_len, None), (query_len, span, bias_long)):
            one, two = [attend(first, count, lane, half, bias) for half in halves]
            for part in range(3):
                both = jnp.concatenate([one[part], two[part]], axis=1)
                out_ref[pl.ds(first, count), pl.ds(lane + part * D, 128)] = low(both)
        return carry

    lax.fori_loop(0, HEADS // 2, pair, 0)


def attention_call(kernel, lens, arrays, out_width, query_len, span, micro_count, cost):
    length = query_len + span
    return pl.pallas_call(
        functools.partial(kernel, query_len=query_len, span=span),
        out_shape=jax.ShapeDtypeStruct((micro_count * length, out_width), bf16),
        grid_spec=pltpu.PrefetchScalarGridSpec(
            num_scalar_prefetch=1,
            grid=(micro_count,),
            in_specs=[
                pl.BlockSpec((length, member.shape[1]), lambda micro, lens: (micro, 0))
                for member in arrays
            ],
            out_specs=pl.BlockSpec((length, out_width), lambda micro, lens: (micro, 0)),
        ),
        compiler_params=pltpu.CompilerParams(vmem_limit_bytes=48 * 1024 * 1024),
        cost_estimate=pl.CostEstimate(
            flops=cost * micro_count * HEADS * span * span * HDIM * 2,
            bytes_accessed=micro_count * length * (out_width + 3 * D) * 2,
            transcendentals=micro_count * HEADS * span * span,
        ),
    )(lens, *arrays)


def share_all(value, axes, count):
    spread = jnp.broadcast_to(value[None], (count,) + value.shape)
    return lax.all_to_all(spread, axes, 0, 0, tiled=True)


def swap(value, axis, size, bit):
    return lax.ppermute(value, axis, [(place, place ^ bit) for place in range(size)])


def reduce_rows(whole, narrow, blocks, wire):
    place = lax.axis_index("narrow")
    low_bit, upper = place & 1, place // 2
    width, depth = whole.shape[0] // narrow, whole.shape[1]
    pairs = narrow // 2

    def rows_of(offset, bit):
        return lax.dynamic_slice_in_dim(whole, (2 * (upper ^ offset) + bit) * width, width, axis=0)

    totals = [None] * pairs
    for offset in reversed(range(pairs)):
        got = swap(rows_of(offset, 1 - low_bit).astype(wire), "narrow", narrow, 1)
        totals[offset] = rows_of(offset, low_bit) + got.astype(f32)
    half = pairs // 2
    while half:
        for offset in range(half):
            got = swap(totals[offset + half].astype(wire), "narrow", narrow, 2 * half)
            totals[offset] = totals[offset] + got.astype(f32)
        half = half // 2
    parts = totals[0].astype(wire).reshape(blocks, -1, depth)
    parts = lax.all_to_all(parts, "blk", 0, 0, tiled=True)
    return jnp.sum(parts.astype(f32), axis=0)


def sum_narrow(value, narrow):
    place = lax.axis_index("narrow")
    if narrow & (narrow - 1):
        return lax.psum(value, "narrow")
    halves = value.reshape(2, value.shape[0] // 2, value.shape[1])
    low_bit = place & 1
    mine = lax.dynamic_index_in_dim(halves, low_bit, 0, keepdims=False)
    other = lax.dynamic_index_in_dim(halves, 1 - low_bit, 0, keepdims=False)
    total = mine + swap(other, "narrow", narrow, 1)
    bit = 2
    while bit < narrow:
        total = total + swap(total, "narrow", narrow, bit)
        bit = bit * 2
    other = swap(total, "narrow", narrow, 1)
    first = jnp.where(low_bit == 0, total, other)
    second = jnp.where(low_bit == 0, other, total)
    return jnp.concatenate([first, second], axis=0)


def adam_step(weight, first, second, gradient, rate):
    first_new = beta_one * first + (1.0 - beta_one) * gradient
    second_new = beta_two * second + (1.0 - beta_two) * gradient * gradient
    update = (
        first_new
        / (1.0 - beta_one**STEP)
        / (jnp.sqrt(second_new / (1.0 - beta_two**STEP)) + adam_eps)
    )
    return (weight - rate * (update + weight_decay * weight), first_new, second_new)


def split_into(value, left_ref, right_ref, first):
    count, size = value.shape
    high = low(value)
    rest = low(value - high.astype(f32))
    rows = pl.ds(first, count)
    if left_ref is not None:
        left_ref[rows, 0:size] = high
        left_ref[rows, size : 2 * size] = high
        left_ref[rows, 2 * size : 3 * size] = rest
    if right_ref is not None:
        right_ref[rows, :] = high
        right_ref[pl.ds(first + size, count), :] = rest
        right_ref[pl.ds(first + 2 * size, count), :] = high


def chain_kernel(*refs):
    refs = [refs[side::2] for side in (0, 1)]

    def steps(size):
        return [(first, min(256, size - first)) for first in range(0, size, 256)]

    for gram_in, rows_in, _, gram, rows, half, gram_l, gram_r, poly_l, poly_r, half_l, rows_l in refs:
        size, count = gram.shape[0], rows.shape[0]
        diagonal = lax.broadcasted_iota(jnp.int32, (size, size), 0) == lax.broadcasted_iota(
            jnp.int32, (size, size), 1
        )
        trace = jnp.sum(jnp.where(diagonal, gram_in[...], 0.0), axis=(0, 1), keepdims=True)
        scale = 1.0 / (jnp.sqrt(trace) + 1e-07)
        for first, step in steps(size):
            block = gram_in[pl.ds(first, step), :] * (scale * scale)
            gram[pl.ds(first, step), :] = block
            split_into(block, gram_l, gram_r, first)
        for first, step in steps(count):
            block = rows_in[pl.ds(first, step), :] * scale
            rows[pl.ds(first, step), :] = block
            split_into(block, rows_l, None, first)

    def advance(last):
        for _, _, out, gram, rows, half, gram_l, gram_r, poly_l, poly_r, half_l, rows_l in refs:
            size, count = gram.shape[0], rows.shape[0]
            for first, step in steps(size):
                here = pl.ds(first, step)
                square = dot_nn(gram_l[here, :], gram_r[...])
                poly = newton_two * gram[here, :] + newton_three * square
                split_into(poly, poly_l, poly_r, first)
            if not last:
                for first, step in steps(size):
                    here = pl.ds(first, step)
                    block = newton_one * gram[here, :] + dot_nn(poly_l[here, :], gram_r[...])
                    half[here, :] = block
                    split_into(block, half_l, None, first)
            for first, step in steps(count):
                here = pl.ds(first, step)
                block = newton_one * rows[here, :] + dot_nn(rows_l[here, :], poly_r[...])
                if last:
                    out[here, :] = block.astype(out.dtype)
                else:
                    rows[here, :] = block
                    split_into(block, rows_l, None, first)
            if not last:
                for first, step in steps(size):
                    here = pl.ds(first, step)
                    block = newton_one * half[here, :] + dot_nn(half_l[here, :], poly_r[...])
                    gram[here, :] = block
                    split_into(block, gram_l, gram_r, first)

    def turn(_, carry):
        advance(False)
        return carry

    lax.fori_loop(0, 4, turn, 0)
    advance(True)


def newton_chains(gram, rows, gram_small, rows_small):
    scratch = []
    sizes = ((gram.shape[0], rows.shape[0]), (gram_small.shape[0], rows_small.shape[0]))
    shapes = [
        [((size, size), f32), ((count, size), f32), ((size, size), f32)]
        + [((size, 3 * size), bf16), ((3 * size, size), bf16)] * 2
        + [((size, 3 * size), bf16), ((count, 3 * size), bf16)]
        for size, count in sizes
    ]
    scratch = [pltpu.VMEM(*shape) for pair in zip(*shapes) for shape in pair]
    whole = pl.BlockSpec(memory_space=pltpu.VMEM)
    flops = sum(2 * 3 * (13 * size + 5 * count) * size * size for size, count in sizes)
    return pl.pallas_call(
        chain_kernel,
        out_shape=(
            jax.ShapeDtypeStruct(rows.shape, bf16),
            jax.ShapeDtypeStruct(rows_small.shape, f32),
        ),
        in_specs=[whole] * 4,
        out_specs=(whole, whole),
        scratch_shapes=scratch,
        compiler_params=pltpu.CompilerParams(vmem_limit_bytes=56 * 1024 * 1024),
        cost_estimate=pl.CostEstimate(flops=flops, bytes_accessed=8 * gram.size, transcendentals=0),
    )(gram, gram_small, rows, rows_small)


def body(
    query_ids,
    passage_ids,
    passage_len,
    positives,
    domains,
    table,
    table_m,
    table_v,
    pos_table,
    pos_m,
    pos_v,
    vector,
    vector_m,
    vector_v,
    w_qkv,
    m_qkv,
    w_attn,
    m_attn,
    w_in,
    m_in,
    w_out,
    m_out,
    w_proj,
    m_proj,
):
    blocks = lax.axis_size("blk")
    narrow = lax.axis_size("narrow")
    devices = blocks * narrow
    both = ("blk", "narrow")
    myself = lax.axis_index("blk")
    shard_rows = table.shape[0]
    micro_count, _, query_len = query_ids.shape
    span = passage_ids.shape[2]
    length = query_len + span
    tokens = micro_count * length

    side = D // narrow
    vector_cols = vector.shape[1] // side
    small = jnp.concatenate(
        [
            low(pos_table).T,
            low(w_proj).T,
            low(vector).reshape(side, vector_cols),
            jnp.zeros((side, 128 - vector_cols), bf16),
        ],
        axis=1,
    )

    def gather(shard):
        return lax.all_gather(shard, "narrow", axis=0, tiled=True)

    small = gather(small)
    qkv_t = gather(low(w_qkv).T)
    attn_t = gather(low(w_attn).T)
    in_t = gather(low(w_in).T)
    out_t = gather(low(w_out).T)
    pos = small[:, :span].T.astype(f32)
    proj_t = small[:, span : span + VDIM]
    gains = small[:, span + VDIM : span + VDIM + vector_cols].reshape(-1).astype(f32)
    bounds = [0, D, 2 * D, 3 * D, 4 * D, 5 * D, 6 * D, 7 * D, 7 * D + FF, 8 * D + FF, 9 * D + FF]
    bounds = bounds + [10 * D + FF]
    pieces = [gains[None, bounds[index] : bounds[index + 1]] for index in range(11)]
    qkv_bias = jnp.concatenate([pieces[2], jnp.zeros_like(pieces[2]), pieces[3]], axis=1)

    slots = round_up(SLOT_CAPS.get(shard_rows, tokens), 8)
    ids = jnp.concatenate([query_ids[:, 0], passage_ids[:, 0]], axis=1).reshape(tokens)
    owner = ids // shard_rows
    local_id = ids - owner * shard_rows
    is_owner = owner[:, None] == jnp.arange(devices, dtype=jnp.int32)[None]
    before = jnp.arange(tokens)[:, None] > jnp.arange(tokens)[None]
    earlier = dot_nn(before.astype(bf16), is_owner.astype(bf16))
    rank = jnp.sum(jnp.where(is_owner, earlier, 0.0), axis=1).astype(jnp.int32)
    place = owner * slots + rank
    picks = (place[:, None] == jnp.arange(devices * slots, dtype=jnp.int32)[None]).astype(bf16)
    picks = lax.optimization_barrier(picks)
    digits = jnp.stack([local_id // 32, local_id % 32], axis=1).astype(bf16)
    asked = dot_tn(digits, picks)
    asked = (asked[0] * 32.0 + asked[1]).astype(jnp.int32).reshape(devices, slots)
    wanted = lax.all_to_all(asked, both, 0, 0, tiled=True).reshape(devices * slots)
    chosen = (wanted[:, None] == jnp.arange(shard_rows, dtype=jnp.int32)[None]).astype(bf16)
    chosen = lax.optimization_barrier(chosen)
    sent_rows = low(dot_nn(chosen, low(table))).reshape(devices, slots, D)
    got_rows = lax.all_to_all(sent_rows, both, 0, 0, tiled=True).reshape(devices * slots, D)
    token_rows = dot_nn(picks, got_rows)

    lens = passage_len[:, 0]
    pos_rows = jnp.concatenate([pos[:query_len], pos] * micro_count, axis=0)
    x, x_hat, x_scale = norm_forward(token_rows + pos_rows, pieces[0], pieces[1])
    x_low = low(x)
    qkv = low(dot_nt(x_low, qkv_t) + qkv_bias)
    context = attention_call(
        attention_forward_kernel, lens, (qkv,), D, query_len, span, micro_count, 2
    )
    h, h_hat, h_scale = norm_forward(
        x + dot_nt(context, attn_t) + pieces[4], pieces[5], pieces[6]
    )
    h_low = low(h)
    wide = dot_nt(h_low, in_t) + pieces[7]
    wide = lax.optimization_barrier(wide)
    gelu_value, gelu_slope = gelu_parts(wide)
    f_low, gelu_slope = lax.optimization_barrier((low(gelu_value), gelu_slope))
    o, o_hat, o_scale = norm_forward(h + dot_nn(f_low, out_t) + pieces[8], pieces[9], pieces[10])
    o_low = low(o)
    e = dot_nn(o_low, proj_t)
    e_scale = lax.rsqrt(jnp.sum(e * e, axis=-1, keepdims=True) + 1e-06)
    vecs = low(e * e_scale).reshape(micro_count, length, VDIM)

    query_vecs = vecs[:, :query_len]
    passage_vecs = vecs[:, query_len:]
    cycle = share_all(query_vecs.reshape(micro_count * query_len, VDIM), "blk", blocks)
    cycle = cycle.reshape(blocks, micro_count, query_len, VDIM).transpose(1, 0, 2, 3)
    cycle = cycle.reshape(micro_count, blocks * query_len, VDIM)
    usable = jnp.arange(span)[None] < lens[:, None]
    sims = jnp.einsum("mik,mjk->mij", cycle, passage_vecs, preferred_element_type=f32)
    scaled = jnp.where(usable[:, None, :], sims / smoothing, masked)
    summit = jnp.max(scaled, axis=-1, keepdims=True)
    expvals = jnp.exp(scaled - summit)
    totals = jnp.sum(expvals, axis=-1, keepdims=True)
    smooth = smoothing * (summit[..., 0] + jnp.log(totals[..., 0]))
    scores = jnp.sum(smooth.reshape(micro_count, blocks, query_len), axis=-1)
    every = share_all(scores.reshape(1, micro_count * blocks), "blk", blocks)
    every = every.reshape(blocks, micro_count, blocks).transpose(1, 0, 2)
    labels = domains[:, 0]
    targets = positives[:, 0]
    spots = jnp.arange(blocks, dtype=jnp.int32)
    chosen_label = jnp.sum(
        jnp.where(targets[:, :, None] == spots[None, None], labels[:, None, :], 0), axis=-1
    )
    allowed = labels[:, :, None] == chosen_label[:, None, :]
    hits = targets[:, None, :] == spots[None, :, None]
    permitted = jnp.where(allowed, every, masked)
    peak = jnp.max(permitted, axis=1, keepdims=True)
    mass = jnp.sum(jnp.where(allowed, jnp.exp(every - peak), 0.0), axis=1, keepdims=True)
    log_total = peak + jnp.log(mass)
    matched = jnp.sum(jnp.where(hits, every, 0.0), axis=1)
    own = spots == myself
    loss_part = jnp.sum(jnp.where(own[None], log_total[:, 0] - matched, 0.0))
    d_every = jnp.where(allowed, jnp.exp(every - log_total), 0.0) - hits.astype(f32)
    d_scores = jnp.sum(jnp.where(own[None, :, None], d_every, 0.0), axis=1)
    d_tokens = jnp.broadcast_to(d_scores[:, :, None], (micro_count, blocks, query_len))
    d_sims = low(d_tokens.reshape(micro_count, blocks * query_len, 1) * (expvals / totals))
    d_passage = jnp.einsum("mij,mik->mjk", d_sims, cycle, preferred_element_type=f32)
    d_cycle = jnp.einsum("mij,mjk->mik", d_sims, passage_vecs, preferred_element_type=f32)
    d_cycle = d_cycle.reshape(micro_count, blocks, query_len, VDIM).transpose(1, 0, 2, 3)
    d_query = jnp.sum(lax.all_to_all(d_cycle, "blk", 0, 0, tiled=True), axis=0)
    d_vecs = jnp.concatenate([d_query, d_passage], axis=1).reshape(tokens, VDIM)

    def summed(left, right):
        return reduce_rows(dot_tn(left, right), narrow, blocks, bf16)

    def column_sum(values):
        return jnp.sum(values, axis=0)

    d_vecs = low(d_vecs).astype(f32)
    inner = jnp.sum(e * d_vecs, axis=-1, keepdims=True)
    d_e = low(e_scale * d_vecs - e * (e_scale * e_scale * e_scale * inner))
    g_proj = dot_tn(o_low, d_e)
    d_o = low(dot_nt(d_e, proj_t)).astype(f32)
    g_gain_o, g_shift_o = column_sum(d_o * o_hat), column_sum(d_o)
    d_sum_o = norm_backward(d_o, o_hat, o_scale, pieces[9])
    g_bias_out = column_sum(d_sum_o)
    d_y = low(d_sum_o)
    g_out = summed(f_low, d_y)
    d_f = low(dot_nt(d_y, out_t)).astype(f32)
    d_wide = d_f * gelu_slope
    g_bias_in = column_sum(d_wide)
    d_wide = lax.optimization_barrier(low(d_wide))
    g_in = summed(d_wide, h_low)
    d_h = d_sum_o + low(dot_nn(d_wide, in_t)).astype(f32)
    g_gain_h, g_shift_h = column_sum(d_h * h_hat), column_sum(d_h)
    d_sum_h = norm_backward(d_h, h_hat, h_scale, pieces[5])
    g_bias_attn = column_sum(d_sum_h)
    d_a = low(d_sum_h)
    g_attn = summed(d_a, context)
    d_context = low(dot_nn(d_a, attn_t))
    d_qkv = attention_call(
        attention_backward_kernel,
        lens,
        (qkv, d_context),
        3 * D,
        query_len,
        span,
        micro_count,
        5,
    )
    g_qkv = summed(d_qkv, x_low)
    g_bias_qkv = column_sum(d_qkv.astype(f32))
    d_x = d_sum_h + low(dot_nn(d_qkv, qkv_t)).astype(f32)
    g_gain_x, g_shift_x = column_sum(d_x * x_hat), column_sum(d_x)
    d_rows = norm_backward(d_x, x_hat, x_scale, pieces[0])
    d_rows = lax.optimization_barrier(d_rows)

    back_rows = low(dot_tn(picks, low(d_rows))).reshape(devices, slots, D)
    back_rows = lax.all_to_all(back_rows, both, 0, 0, tiled=True).reshape(devices * slots, D)
    table_grad = dot_tn(chosen, back_rows)
    d_micro = d_rows.reshape(micro_count, length, D)
    g_pos = jnp.sum(d_micro[:, query_len:], axis=0)
    g_pos = jnp.concatenate(
        [g_pos[:query_len] + jnp.sum(d_micro[:, :query_len], axis=0), g_pos[query_len:]], axis=0
    )
    g_vector = jnp.concatenate(
        [
            g_gain_x,
            g_shift_x,
            g_bias_qkv[:D],
            g_bias_qkv[2 * D :],
            g_bias_attn,
            g_gain_h,
            g_shift_h,
            g_bias_in,
            g_bias_out,
            g_gain_o,
            g_shift_o,
        ]
    )
    tail_spare = round_up(span + VDIM + vector_cols + 1, 128) - (span + VDIM + vector_cols + 1)
    tail = jnp.concatenate(
        [
            g_pos.T,
            g_proj,
            g_vector.reshape(D, vector_cols),
            g_bias_attn[:, None],
            jnp.zeros((D, tail_spare), f32),
        ],
        axis=1,
    )
    g_tail = reduce_rows(tail, narrow, blocks, f32)

    def square_sum(values):
        values = values.astype(f32)
        return jnp.sum(values * values)

    local_square = (
        square_sum(table_grad)
        + square_sum(g_out)
        + square_sum(g_in)
        + square_sum(g_qkv)
        + square_sum(g_attn)
        + square_sum(g_tail[:, : span + VDIM + vector_cols])
    )
    lane = jnp.arange(128)[None]
    pair = jnp.where(lane == 0, local_square, jnp.where(lane == 1, loss_part, 0.0))
    sums = jnp.sum(share_all(pair, both, devices), axis=(0, 1))
    loss = sums[1]
    grad_norm = jnp.sqrt(sums[0])
    factor = jnp.minimum(1.0, clip_limit / (grad_norm + 1e-06))

    wide_rows = g_out.shape[0]
    attn_rows = g_attn.shape[0]
    g_out, g_in, g_qkv, g_attn, g_tail = (
        low(member) for member in (g_out, g_in, g_qkv, g_attn, g_tail)
    )
    packed = [g_out, g_in, g_qkv, g_attn, g_tail]
    flat = jnp.concatenate([member.reshape(-1, 128) for member in packed], axis=0)
    complete = lax.all_gather(flat, "blk", axis=0, tiled=False)
    parts, first = [], 0
    for member in packed:
        count = member.size // 128
        parts.append(complete[:, first : first + count])
        first += count
    grad_out = parts[0].reshape(-1, D).T.astype(f32)
    grad_in = parts[1].reshape(-1, D).T.astype(f32)
    grad_qkv = parts[2].reshape(-1, D).T.astype(f32)
    grad_attn = parts[3].reshape(-1, D).T.astype(f32)
    tail_all = parts[4].reshape(side, tail.shape[1])
    grad_pos = tail_all[:, :span].T.astype(f32)
    grad_proj = tail_all[:, span : span + VDIM].T.astype(f32)
    rest = tail_all[:, span + VDIM : span + VDIM + vector_cols + 1].astype(f32)
    grad_vector = rest[:, :vector_cols].reshape(1, -1)
    grad_bias = rest[:, vector_cols].reshape(1, -1)

    per = blocks // MATRICES
    turn_of = myself // per

    def padded(rows):
        return jnp.pad(rows, ((0, 0), (0, wide_rows - rows.shape[1]), (0, 0)))

    def blocked(shard):
        return padded(shard.T.reshape(blocks, -1, D))

    old = jnp.stack([blocked(member) for member in (m_qkv, m_attn, m_in, m_out)])
    old = lax.dynamic_index_in_dim(old, turn_of, 0, keepdims=False).reshape(-1, D)
    proj_rows = g_tail[:, span : span + VDIM]
    proj_fill = round_up(proj_rows.size // 128, 8) * 128
    proj_flat = jnp.pad(proj_rows.reshape(-1), (0, round_up(proj_fill, 8 * D) - proj_rows.size))
    proj_flat = proj_flat.reshape(-1, D)
    sends = [padded(member[None])[0] for member in (g_qkv, g_attn, g_in, g_out)]
    sends = jnp.stack([jnp.concatenate([member, proj_flat], axis=0) for member in sends])
    sends = jnp.repeat(sends, per, axis=0)
    taken = lax.all_to_all(sends, "blk", 0, 0, tiled=True)
    moment = muon_moment * old + factor * taken[:, :wide_rows].reshape(-1, D).astype(f32)
    proj_taken = taken[:, wide_rows:].reshape(blocks, -1)[:, : proj_rows.size].reshape(-1, VDIM)
    proj_moment = muon_moment * m_proj.T + factor * proj_taken.astype(f32)

    def gram_of(rows):
        return lax.dot_general(
            rows,
            rows,
            (((0,), (0,)), ((), ())),
            precision=lax.Precision.HIGH,
            preferred_element_type=f32,
        )

    gram_proj = gram_of(proj_moment).reshape(-1)
    gram_proj = jnp.pad(gram_proj, (0, round_up(gram_proj.size, 16 * D) - gram_proj.size))
    grams = jnp.concatenate([gram_of(moment), gram_proj.reshape(-1, D)], axis=0)
    grams = sum_narrow(grams, narrow)
    gram_proj = grams[D:].reshape(-1)[: VDIM * VDIM].reshape(VDIM, VDIM)
    share = moment.shape[0] // per
    mine = lax.dynamic_slice_in_dim(moment, (myself % per) * share, share, axis=0)
    ortho, ortho_proj = newton_chains(grams[:D], mine, gram_proj, proj_moment)
    ortho = lax.all_gather(ortho, "blk", axis=0, tiled=False)
    ortho = ortho.reshape(MATRICES, blocks, wide_rows, D)

    def unblocked(index, rows):
        return ortho[index, :, :rows].reshape(-1, D).T.astype(f32)

    orthos = (
        unblocked(0, g_qkv.shape[0]),
        unblocked(1, attn_rows),
        unblocked(2, wide_rows),
        unblocked(3, wide_rows),
        ortho_proj.T,
    )

    table_new, table_m_new, table_v_new = adam_step(
        table, table_m, table_v, factor * table_grad, adam_rate
    )
    pos_new, pos_m_new, pos_v_new = adam_step(
        pos_table, pos_m, pos_v, factor * grad_pos, adam_rate
    )
    vector_new, vector_m_new, vector_v_new = adam_step(
        vector, vector_m, vector_v, factor * grad_vector, vector_rate
    )
    masters = (w_qkv, w_attn, w_in, w_out, w_proj)
    rates = (muon_rate, attn_rate, muon_rate, muon_rate, muon_rate)
    olds = (m_qkv, m_attn, m_in, m_out, m_proj)
    grads = (grad_qkv, grad_attn, grad_in, grad_out, grad_proj)
    moments = [muon_moment * before + factor * grad for before, grad in zip(olds, grads)]
    updated = []
    for weight, ortho_part, rate in zip(masters, orthos, rates):
        long_side = max(weight.shape[0], weight.shape[1] * narrow)
        updated.append(weight - rate * (0.2 * long_side**0.5 * ortho_part + weight_decay * weight))
    return (
        loss,
        grad_norm,
        table_new,
        table_m_new,
        table_v_new,
        pos_new,
        pos_m_new,
        pos_v_new,
        vector_new,
        vector_m_new,
        vector_v_new,
        updated[0],
        moments[0],
        updated[1],
        moments[1],
        updated[2],
        moments[2],
        updated[3],
        moments[3],
        updated[4],
        moments[4],
        factor * grad_bias,
    )


def solution(mesh):
    ids = P(None, ("blk", "narrow"), None)
    rows = P(("blk", "narrow"), None)
    cols = P(None, "narrow")
    group = P(None, "narrow", None)
    in_specs = (ids, ids, P(None, ("blk", "narrow")), group, group) + (rows,) * 3 + (cols,) * 16
    out_specs = (P(), P()) + (rows,) * 3 + (cols,) * 17
    return jax.shard_map(body, mesh=mesh, in_specs=in_specs, out_specs=out_specs, check_vma=False)
```

```python
import functools

import jax
import jax.numpy as jnp
from jax import lax
from jax.experimental import pallas as pl
from jax.experimental.pallas import tpu as pltpu
from jax.sharding import PartitionSpec as P

D = 768
HEADS = 12
HDIM = 64
FF = 3072
VDIM = 128
STEP = 10
MATRICES = 4

norm_eps = 1e-12
smoothing = 0.1
masked = -1e30
newton_one = 3.4445
newton_two = -4.775
newton_three = 2.0315
muon_rate = 0.1
attn_rate = 1.0
muon_moment = 0.95
weight_decay = 0.01
adam_rate = 0.02
vector_rate = 0.25
beta_one = 0.9
beta_two = 0.95
adam_eps = 1e-08
clip_limit = 0.05

bf16 = jnp.bfloat16
f32 = jnp.float32
SLOT_CAPS = {960: 36, 120: 7}


def round_up(value, step):
    return -(-value // step) * step


def dot_nn(left, right):
    return lax.dot_general(left, right, (((1,), (0,)), ((), ())), preferred_element_type=f32)


def dot_nt(left, right):
    return lax.dot_general(left, right, (((1,), (1,)), ((), ())), preferred_element_type=f32)


def dot_tn(left, right):
    return lax.dot_general(left, right, (((0,), (0,)), ((), ())), preferred_element_type=f32)


def low(values):
    return values.astype(bf16)


def norm_forward(values, gain, shift):
    centred = values - jnp.mean(values, axis=-1, keepdims=True)
    spread = jnp.mean(centred * centred, axis=-1, keepdims=True)
    scale = lax.rsqrt(spread + norm_eps)
    hat = centred * scale
    return hat * gain + shift, hat, scale


def norm_backward(grad, hat, scale, gain):
    d_hat = grad * gain
    first = jnp.mean(d_hat, axis=-1, keepdims=True)
    second = jnp.mean(d_hat * hat, axis=-1, keepdims=True)
    return scale * (d_hat - first - hat * second)


def gelu_parts(values):
    cdf = 0.5 * (1.0 + lax.erf(values * (0.5**0.5)))
    density = jnp.exp(-0.5 * values * values) * 0.3989422804014327
    return values * cdf, cdf + values * density


def attention_forward_kernel(
    lens_ref, qkv_ref, out_ref, norm_ref, scores_one, scores_two, share_one, share_two, *, query_len, span
):
    used = lens_ref[pl.program_id(0)]
    bias_long = jnp.where(lax.broadcasted_iota(jnp.int32, (1, span), 1) < used, 0.0, masked)
    bias_short = jnp.zeros((1, query_len), f32)
    lane_of = lax.broadcasted_iota(jnp.int32, (16, 128), 1)
    norm_ref[...] = jnp.zeros_like(norm_ref)

    def attend(first, count, lane, half, bias, head, scores_ref, share_ref):
        rows, span_of = pl.ds(first, count), pl.ds(0, count)
        queries = qkv_ref[rows, pl.ds(lane, 128)][:, half] * bf16(HDIM**-0.5)
        keys = qkv_ref[rows, pl.ds(lane + D, 128)][:, half]
        values = qkv_ref[rows, pl.ds(lane + 2 * D, 128)][:, half]
        scores_ref[span_of, span_of] = dot_nt(queries, keys)
        for step in range(0, count, 16):
            here = pl.ds(step, 16)
            scores = scores_ref[here, span_of] + bias
            peak = jnp.max(scores, axis=-1, keepdims=True)
            exponent = jnp.exp(scores - peak)
            total = jnp.sum(exponent, axis=-1, keepdims=True)
            share_ref[here, span_of] = low(exponent * (1.0 / total))
            there = pl.ds(first + step, 16)
            norm_ref[there, :] = jnp.where(lane_of == head, peak + jnp.log(total), norm_ref[there, :])
        return dot_nn(share_ref[span_of, span_of], values)

    def pair(index, carry):
        lane = pl.multiple_of(index * 128, 128)
        for first, count, bias in ((0, query_len, bias_short), (query_len, span, bias_long)):
            one = attend(
                first, count, lane, slice(0, HDIM), bias, 2 * index, scores_one, share_one
            )
            two = attend(
                first, count, lane, slice(HDIM, 128), bias, 2 * index + 1, scores_two, share_two
            )
            out_ref[pl.ds(first, count), pl.ds(lane, 128)] = low(jnp.concatenate([one, two], axis=1))
        return carry

    lax.fori_loop(0, HEADS // 2, pair, 0)


def attention_forward(lens, qkv, query_len, span):
    length = query_len + span
    tokens = qkv.shape[0]
    micro_count = tokens // length
    block = pl.BlockSpec((length, 3 * D), lambda micro, lens: (micro, 0))
    square = [pltpu.VMEM((span, span), f32)] * 2 + [pltpu.VMEM((span, span), bf16)] * 2
    return pl.pallas_call(
        functools.partial(attention_forward_kernel, query_len=query_len, span=span),
        out_shape=(
            jax.ShapeDtypeStruct((tokens, D), bf16),
            jax.ShapeDtypeStruct((tokens, 128), f32),
        ),
        grid_spec=pltpu.PrefetchScalarGridSpec(
            num_scalar_prefetch=1,
            grid=(micro_count,),
            in_specs=[block],
            out_specs=(
                pl.BlockSpec((length, D), lambda micro, lens: (micro, 0)),
                pl.BlockSpec((length, 128), lambda micro, lens: (micro, 0)),
            ),
            scratch_shapes=square,
        ),
        compiler_params=pltpu.CompilerParams(vmem_limit_bytes=48 * 1024 * 1024),
        cost_estimate=pl.CostEstimate(
            flops=8 * micro_count * HEADS * span * span * HDIM,
            bytes_accessed=tokens * 8 * D,
            transcendentals=micro_count * HEADS * span * span,
        ),
    )(lens, qkv)


def attention_backward_kernel(
    lens_ref,
    qkv_ref,
    grad_ref,
    norm_ref,
    inner_ref,
    out_ref,
    scores_one,
    scores_two,
    slopes_one,
    slopes_two,
    share_one,
    share_two,
    d_one,
    d_two,
    *,
    query_len,
    span,
):
    used = lens_ref[pl.program_id(0)]
    bias_long = jnp.where(lax.broadcasted_iota(jnp.int32, (span, 1), 0) < used, 0.0, masked)
    bias_short = jnp.zeros((query_len, 1), f32)

    def attend(first, count, lane, half, bias, head, scores_ref, slopes_ref, share_ref, d_ref):
        rows, span_of = pl.ds(first, count), pl.ds(0, count)
        queries = qkv_ref[rows, pl.ds(lane, 128)][:, half] * bf16(HDIM**-0.5)
        keys = qkv_ref[rows, pl.ds(lane + D, 128)][:, half]
        values = qkv_ref[rows, pl.ds(lane + 2 * D, 128)][:, half]
        grads = grad_ref[rows, pl.ds(lane, 128)][:, half]
        lanes = slice(0, count) if first else slice(span, span + count)
        norm = norm_ref[0, pl.ds(head, 1), :][:, lanes]
        inner = inner_ref[0, pl.ds(head, 1), :][:, lanes]
        scores_ref[span_of, span_of] = dot_nt(keys, queries)
        slopes_ref[span_of, span_of] = dot_nt(values, grads)
        for step in range(0, count, 16):
            here = pl.ds(step, 16)
            scores = scores_ref[here, span_of] + bias[step : step + 16]
            share = jnp.exp(scores - norm)
            share_ref[here, span_of] = low(share)
            d_ref[here, span_of] = low(share * (slopes_ref[here, span_of] - inner))
        d_scores = d_ref[span_of, span_of]
        d_values = dot_nn(share_ref[span_of, span_of], grads)
        d_keys = dot_nn(d_scores, queries)
        d_queries = dot_tn(d_scores, keys) * HDIM**-0.5
        return d_queries, d_keys, d_values

    def pair(index, carry):
        lane = pl.multiple_of(index * 128, 128)
        for first, count, bias in ((0, query_len, bias_short), (query_len, span, bias_long)):
            one = attend(
                first,
                count,
                lane,
                slice(0, HDIM),
                bias,
                2 * index,
                scores_one,
                slopes_one,
                share_one,
                d_one,
            )
            two = attend(
                first,
                count,
                lane,
                slice(HDIM, 128),
                bias,
                2 * index + 1,
                scores_two,
                slopes_two,
                share_two,
                d_two,
            )
            for part in range(3):
                both = jnp.concatenate([one[part], two[part]], axis=1)
                out_ref[pl.ds(first, count), pl.ds(lane + part * D, 128)] = low(both)
        return carry

    lax.fori_loop(0, HEADS // 2, pair, 0)


def attention_backward(lens, qkv, grad, norm, inner, query_len, span):
    length = query_len + span
    tokens = qkv.shape[0]
    micro_count = tokens // length
    heads = norm.shape[1]

    def block(width):
        return pl.BlockSpec((length, width), lambda micro, lens: (micro, 0))

    row = pl.BlockSpec((1, heads, length), lambda micro, lens: (micro, 0, 0))
    square = [pltpu.VMEM((span, span), f32)] * 4 + [pltpu.VMEM((span, span), bf16)] * 4
    return pl.pallas_call(
        functools.partial(attention_backward_kernel, query_len=query_len, span=span),
        out_shape=jax.ShapeDtypeStruct((tokens, 3 * D), bf16),
        grid_spec=pltpu.PrefetchScalarGridSpec(
            num_scalar_prefetch=1,
            grid=(micro_count,),
            in_specs=[block(3 * D), block(D), row, row],
            out_specs=block(3 * D),
            scratch_shapes=square,
        ),
        compiler_params=pltpu.CompilerParams(vmem_limit_bytes=48 * 1024 * 1024),
        cost_estimate=pl.CostEstimate(
            flops=20 * micro_count * HEADS * span * span * HDIM,
            bytes_accessed=tokens * 14 * D,
            transcendentals=micro_count * HEADS * span * span,
        ),
    )(lens, qkv, grad, norm, inner)


def update_kernel(*refs, rate, scale):
    count = len(refs) // 3
    for weight, ortho, out in zip(refs[:count], refs[count : 2 * count], refs[2 * count :]):
        turned = ortho[...].astype(f32).T
        out[...] = weight[...] - rate * (scale * turned + weight_decay * weight[...])


def update_wide(weights, orthos, rate, scale):
    rows, columns = weights[0].shape
    step = 128
    weight_spec = pl.BlockSpec((rows, step), lambda place: (0, place))
    ortho_spec = pl.BlockSpec((step, rows), lambda place: (place, 0))
    count = len(weights)
    return pl.pallas_call(
        functools.partial(update_kernel, rate=rate, scale=scale),
        grid=(columns // step,),
        in_specs=[weight_spec] * count + [ortho_spec] * count,
        out_specs=(weight_spec,) * count,
        out_shape=(jax.ShapeDtypeStruct((rows, columns), f32),) * count,
        compiler_params=pltpu.CompilerParams(vmem_limit_bytes=32 * 1024 * 1024),
        cost_estimate=pl.CostEstimate(
            flops=4 * count * rows * columns,
            bytes_accessed=10 * count * rows * columns,
            transcendentals=0,
        ),
    )(*weights, *orthos)


def score_kernel(lens_ref, cycle_ref, vecs_ref, share_ref, scores_ref, *, query_len, span):
    micro = pl.program_id(0)
    blocks = cycle_ref.shape[0]
    mine = pl.ds(pl.multiple_of(micro * query_len, query_len), query_len)
    queries = jnp.concatenate([cycle_ref[place, mine, :] for place in range(blocks)], axis=0)
    first = pl.multiple_of(micro * (query_len + span) + query_len, query_len)
    sims = dot_nt(queries, vecs_ref[pl.ds(first, span), :])
    used = lax.broadcasted_iota(jnp.int32, (1, span), 1) < lens_ref[micro]
    scaled = jnp.where(used, sims / smoothing, masked)
    summit = jnp.max(scaled, axis=-1, keepdims=True)
    exponent = jnp.exp(scaled - summit)
    total = jnp.sum(exponent, axis=-1, keepdims=True)
    share_ref[0] = exponent / total
    smooth = smoothing * (summit + jnp.log(total))
    smooth = jnp.broadcast_to(smooth, (blocks * query_len, 128))
    scores_ref[0] = jnp.sum(smooth.reshape(blocks, query_len, 128), axis=1)


def score_forward(lens, cycle, vecs, query_len, span):
    blocks, micro_count = cycle.shape[0], lens.shape[0]
    rows = blocks * query_len
    return pl.pallas_call(
        functools.partial(score_kernel, query_len=query_len, span=span),
        out_shape=(
            jax.ShapeDtypeStruct((micro_count, rows, span), f32),
            jax.ShapeDtypeStruct((micro_count, blocks, 128), f32),
        ),
        grid_spec=pltpu.PrefetchScalarGridSpec(
            num_scalar_prefetch=1,
            grid=(micro_count,),
            in_specs=[
                pl.BlockSpec(cycle.shape, lambda micro, lens: (0, 0, 0)),
                pl.BlockSpec(vecs.shape, lambda micro, lens: (0, 0)),
            ],
            out_specs=(
                pl.BlockSpec((1, rows, span), lambda micro, lens: (micro, 0, 0)),
                pl.BlockSpec((1, blocks, 128), lambda micro, lens: (micro, 0, 0)),
            ),
        ),
        compiler_params=pltpu.CompilerParams(vmem_limit_bytes=48 * 1024 * 1024),
        cost_estimate=pl.CostEstimate(
            flops=2 * micro_count * rows * span * VDIM,
            bytes_accessed=4 * micro_count * rows * span,
            transcendentals=micro_count * rows * span,
        ),
    )(lens, cycle, vecs)


def loss_kernel(
    me_ref,
    every_ref,
    allowed_ref,
    hits_ref,
    share_ref,
    cycle_ref,
    vecs_ref,
    loss_ref,
    passage_ref,
    query_ref,
    *,
    query_len,
    span,
):
    me = me_ref[0]
    blocks = cycle_ref.shape[0]
    micro_count = share_ref.shape[0]
    every = every_ref[...]
    allowed = allowed_ref[...] > 0.0
    peak = jnp.max(jnp.where(allowed, every, masked), axis=0)
    mass = jnp.sum(jnp.where(allowed, jnp.exp(every - peak[None]), 0.0), axis=0)
    log_total = peak + jnp.log(mass)
    matched = jnp.sum(jnp.where(hits_ref[...] > 0.0, every, 0.0), axis=0)
    row = lax.broadcasted_iota(jnp.int32, log_total.shape, 0)
    mine = jnp.where(row % blocks == me, log_total - matched, 0.0)
    loss_ref[...] = jnp.broadcast_to(jnp.sum(mine, axis=0, keepdims=True), loss_ref.shape)
    d_scores = jnp.where(allowed_ref[me] > 0.0, jnp.exp(every_ref[me] - log_total), 0.0)
    d_scores = d_scores - hits_ref[me]
    for micro in range(micro_count):
        own = d_scores[micro * blocks : (micro + 1) * blocks]
        own = jnp.broadcast_to(own[:, None, :], (blocks, query_len, 128))
        own = own.reshape(blocks * query_len, 128)[:, 0:1]
        d_sims = low(own * share_ref[micro])
        here = slice(micro * query_len, (micro + 1) * query_len)
        queries = jnp.concatenate([cycle_ref[place, here, :] for place in range(blocks)], axis=0)
        first = micro * (query_len + span) + query_len
        passage_ref[micro] = dot_tn(d_sims, queries)
        d_queries = dot_nn(d_sims, vecs_ref[first : first + span, :])
        for place in range(blocks):
            rows = slice(place * query_len, (place + 1) * query_len)
            query_ref[place, here, :] = d_queries[rows]


def score_backward(me, every, allowed, hits, share, cycle, vecs, query_len, span):
    micro_count = share.shape[0]
    whole = pl.BlockSpec(memory_space=pltpu.VMEM)
    return pl.pallas_call(
        functools.partial(loss_kernel, query_len=query_len, span=span),
        out_shape=(
            jax.ShapeDtypeStruct((8, 128), f32),
            jax.ShapeDtypeStruct((micro_count, span, VDIM), f32),
            jax.ShapeDtypeStruct(cycle.shape, f32),
        ),
        in_specs=[pl.BlockSpec(memory_space=pltpu.SMEM)] + [whole] * 6,
        out_specs=(whole,) * 3,
        compiler_params=pltpu.CompilerParams(vmem_limit_bytes=48 * 1024 * 1024),
        cost_estimate=pl.CostEstimate(
            flops=4 * share.size * VDIM, bytes_accessed=4 * share.size, transcendentals=0
        ),
    )(me.reshape(1).astype(jnp.int32), every, allowed, hits, share, cycle, vecs)


def tail_kernel(rows_ref, x_ref, hat_ref, qkv_ref, proj_ref, *refs, query_len, span, micro_count):
    out_ref = refs[-1]
    length = query_len + span
    for first in range(0, span, 128):
        block = rows_ref[query_len + first : query_len + first + 128, :]
        for micro in range(1, micro_count):
            start = micro * length + query_len + first
            block = block + rows_ref[start : start + 128, :]
        if first == 0:
            head = rows_ref[0:query_len, :]
            for micro in range(1, micro_count):
                head = head + rows_ref[micro * length : micro * length + query_len, :]
            block = jnp.concatenate([block[:query_len] + head, block[query_len:]], axis=0)
        out_ref[:, first : first + 128] = block.T

    def fold(values):
        return jnp.sum(values.reshape(-1, 8, D), axis=0)

    sums = [jnp.zeros((8, D), f32)] * 4
    for first in range(0, micro_count * length, 32):
        here = pl.ds(first, 32)
        d_x = x_ref[here, :]
        terms = (
            d_x * hat_ref[here, :],
            d_x,
            qkv_ref[here, 0:D].astype(f32),
            qkv_ref[here, 2 * D : 3 * D].astype(f32),
        )
        sums = [total + fold(term) for total, term in zip(sums, terms)]
    sums = [jnp.sum(total, axis=0, keepdims=True) for total in sums]
    for ref in refs[:-1]:
        sums = sums + [ref[:, first : first + D] for first in range(0, ref.shape[1], D)]
    sums.append(jnp.zeros((128 - len(sums), D), f32))
    out_ref[:, span : span + 128] = jnp.concatenate(sums, axis=0).T
    out_ref[:, span + 128 :] = proj_ref[...]


def late_sums(d_rows, d_x, x_hat, d_qkv, g_proj, early, query_len, span, micro_count):
    early = [member.reshape(1, -1) for member in early]
    whole = pl.BlockSpec(memory_space=pltpu.VMEM)
    return pl.pallas_call(
        functools.partial(
            tail_kernel, query_len=query_len, span=span, micro_count=micro_count
        ),
        out_shape=jax.ShapeDtypeStruct((D, span + 128 + VDIM), f32),
        in_specs=[whole] * (5 + len(early)),
        out_specs=whole,
        compiler_params=pltpu.CompilerParams(vmem_limit_bytes=48 * 1024 * 1024),
        cost_estimate=pl.CostEstimate(
            flops=8 * d_rows.size, bytes_accessed=20 * d_rows.size, transcendentals=0
        ),
    )(d_rows, d_x, x_hat, d_qkv, g_proj, *early)


def share_all(value, axes, count):
    spread = jnp.broadcast_to(value[None], (count,) + value.shape)
    return lax.all_to_all(spread, axes, 0, 0, tiled=True)


def swap(value, axis, size, bit):
    return lax.ppermute(value, axis, [(place, place ^ bit) for place in range(size)])


def gather_relative(shard, narrow):
    pieces = {0: shard}
    bit = narrow // 2
    while bit:
        for offset in list(pieces):
            pieces[offset ^ bit] = swap(pieces[offset], "narrow", narrow, bit)
        bit = bit // 2
    return [pieces[offset] for offset in range(narrow)]


def relative(whole, narrow):
    place = lax.axis_index("narrow")
    rows = whole.shape[0] // narrow
    return [
        lax.dynamic_slice_in_dim(whole, (place ^ offset) * rows, rows, axis=0)
        for offset in range(narrow)
    ]


def gram_kernel(factor_ref, old_ref, grad_ref, moment_ref, gram_ref):
    moment = muon_moment * old_ref[...] + factor_ref[0] * grad_ref[...].astype(f32)
    moment_ref[...] = moment
    high, rest = split(moment)
    size = moment.shape[1]
    side = size if gram_ref.shape[0] == size else size // 3

    def part(row):
        left = slice(row, row + side)
        right = slice(row, size)
        return (
            dot_tn(high[:, left], high[:, right])
            + dot_tn(high[:, left], rest[:, right])
            + dot_tn(rest[:, left], high[:, right])
        )

    gram_ref[0:side, :] = part(0)
    if side < size:
        gram_ref[side : 2 * side, 0 : 2 * side] = part(side)
        gram_ref[side : 2 * side, 2 * side : size] = part(2 * side)


def packed_gram(factor, old, grad):
    count, size = old.shape
    whole = pl.BlockSpec(memory_space=pltpu.VMEM)
    packed = size if size < 3 * 128 else 2 * size // 3
    return pl.pallas_call(
        gram_kernel,
        out_shape=(
            jax.ShapeDtypeStruct((count, size), f32),
            jax.ShapeDtypeStruct((packed, size), f32),
        ),
        in_specs=[pl.BlockSpec(memory_space=pltpu.SMEM), whole, whole],
        out_specs=(whole, whole),
        compiler_params=pltpu.CompilerParams(vmem_limit_bytes=48 * 1024 * 1024),
        cost_estimate=pl.CostEstimate(
            flops=4 * count * size * size, bytes_accessed=14 * count * size, transcendentals=0
        ),
    )(factor.reshape(1), old, grad)


def tie(*values):
    return lax.optimization_barrier(values)


class Reduction:
    def __init__(self, sent, kept, narrow, blocks, wire):
        self.narrow, self.blocks, self.wire = narrow, blocks, wire
        self.sent, self.kept = list(sent), list(kept)

    def across_core(self):
        self.got = [swap(member, "narrow", self.narrow, 1) for member in self.sent]

    def prepare(self):
        totals = [kept + got for kept, got in zip(self.kept, self.got)]
        half = len(totals) // 2
        while half > 1:
            for offset in range(half):
                got = swap(totals[offset + half].astype(self.wire), "narrow", self.narrow, 2 * half)
                totals[offset] = totals[offset] + got.astype(f32)
            half = half // 2
        self.kept = totals[0]
        self.outgoing = totals[-1].astype(self.wire)

    def across_narrow(self):
        self.prepare()
        self.send()

    def send(self):
        if self.narrow > 2:
            self.got = swap(self.outgoing, "narrow", self.narrow, 2)
        else:
            self.got = jnp.zeros_like(self.outgoing)

    def total(self):
        return self.kept + self.got.astype(f32)


def sum_everywhere(value, sizes):
    for axis, size in sizes:
        if size <= 8:
            swaps = [swap(value, axis, size, offset) for offset in range(1, size)]
            value = sum(swaps, value)
            continue
        bit = 1
        while bit < size:
            value = value + swap(value, axis, size, bit)
            bit = bit * 2
    return value


def sum_group(value, narrow, per, blocks):
    steps = [("narrow", narrow, 1)]
    steps = steps + [("blk", blocks, 1 << bit) for bit in range(per.bit_length() - 1)]
    for axis, size, bit in steps:
        halves = value.reshape(2, value.shape[0] // 2, value.shape[1])
        mine = (lax.axis_index(axis) // bit) & 1
        sent = lax.dynamic_index_in_dim(halves, 1 - mine, 0, keepdims=False)
        got = swap(sent, axis, size, bit)
        value = lax.dynamic_index_in_dim(halves, mine, 0, keepdims=False) + got
    bit = 2
    while bit < narrow:
        value = value + swap(value, "narrow", narrow, bit)
        bit = bit * 2
    for axis, size, bit in reversed(steps):
        other = swap(value, axis, size, bit)
        lower = (lax.axis_index(axis) // bit) & 1 == 0
        value = jnp.concatenate(
            [jnp.where(lower, value, other), jnp.where(lower, other, value)], axis=0
        )
    return value


def adam_step(weight, first, second, gradient, rate):
    first_new = beta_one * first + (1.0 - beta_one) * gradient
    second_new = beta_two * second + (1.0 - beta_two) * gradient * gradient
    update = (
        first_new
        / (1.0 - beta_one**STEP)
        / (jnp.sqrt(second_new / (1.0 - beta_two**STEP)) + adam_eps)
    )
    return (weight - rate * (update + weight_decay * weight), first_new, second_new)


def split(value):
    high = low(value)
    return high, low(value - high.astype(f32))


def chain_kernel(
    gram_in, rows_in, out, gram, rows, half, gram_l, gram_r, poly_l, poly_r, half_l, rows_l
):
    size, count = gram.shape[0], rows.shape[0]
    parts = 3 if gram_in.shape[0] < size else 1
    side = size // parts

    def put(left_ref, right_ref, value, row, column):
        for piece, first, second in ((value, row, column), (value.T, column, row)):
            high, rest = split(piece)
            width = piece.shape[1]
            if left_ref is not None:
                here = pl.ds(first, piece.shape[0])
                left_ref[here, pl.ds(second, width)] = high
                left_ref[here, pl.ds(size + second, width)] = high
                left_ref[here, pl.ds(2 * size + second, width)] = rest
            if right_ref is not None:
                there = pl.ds(second, width)
                right_ref[pl.ds(first, piece.shape[0]), there] = high
                right_ref[pl.ds(size + first, piece.shape[0]), there] = rest
                right_ref[pl.ds(2 * size + first, piece.shape[0]), there] = high
            if row == column:
                break

    def store(left_ref, right_ref, value, row):
        for place in range(row // side, parts):
            column = place * side
            put(left_ref, right_ref, value[:, column - row : column - row + side], row, column)

    def put_rows(value, first):
        high, rest = split(value)
        here = pl.ds(first, value.shape[0])
        rows_l[here, 0:size] = high
        rows_l[here, size : 2 * size] = high
        rows_l[here, 2 * size : 3 * size] = rest

    def packed(row):
        if parts == 1 or row == 0:
            return gram_in[0:side, :]
        if row == side:
            return gram_in[side : 2 * side, 0 : 2 * side]
        return gram_in[side : 2 * side, 2 * side : size]

    starts = [place * side for place in range(parts)]
    row_steps = [(first, min(256, count - first)) for first in range(0, count, 256)]
    diagonal = lax.broadcasted_iota(jnp.int32, (side, side), 0) == lax.broadcasted_iota(
        jnp.int32, (side, side), 1
    )
    trace = jnp.zeros((1, 1), f32)
    for row in starts:
        block = packed(row)[:, 0:side]
        trace = trace + jnp.sum(jnp.where(diagonal, block, 0.0), axis=(0, 1), keepdims=True)
    scale = 1.0 / (jnp.sqrt(trace) + 1e-07)
    for row in starts:
        block = packed(row) * (scale * scale)
        gram[pl.ds(row, side), pl.ds(row, size - row)] = block
        store(gram_l, gram_r, block, row)
    for first, step in row_steps:
        block = rows_in[pl.ds(first, step), :] * scale
        rows[pl.ds(first, step), :] = block
        put_rows(block, first)

    def product(left_ref, right_ref, row):
        return dot_nn(left_ref[pl.ds(row, side), :], right_ref[:, pl.ds(row, size - row)])

    def advance(last):
        for row in starts:
            here, there = pl.ds(row, side), pl.ds(row, size - row)
            square = product(gram_l, gram_r, row)
            poly = newton_two * gram[here, there] + newton_three * square
            store(None if last else poly_l, poly_r, poly, row)
        if not last:
            for row in starts:
                here, there = pl.ds(row, side), pl.ds(row, size - row)
                block = newton_one * gram[here, there] + product(poly_l, gram_r, row)
                half[here, there] = block
                store(half_l, None, block, row)
        for first, step in row_steps:
            here = pl.ds(first, step)
            block = newton_one * rows[here, :] + dot_nn(rows_l[here, :], poly_r[...])
            if last:
                out[here, :] = block.astype(out.dtype)
            else:
                rows[here, :] = block
                put_rows(block, first)
        if not last:
            for row in starts:
                here, there = pl.ds(row, side), pl.ds(row, size - row)
                block = newton_one * half[here, there] + product(half_l, poly_r, row)
                gram[here, there] = block
                store(gram_l, gram_r, block, row)

    def turn(_, carry):
        advance(False)
        return carry

    lax.fori_loop(0, 4, turn, 0)
    advance(True)


def newton_chain(gram, rows, dtype):
    size, count = rows.shape[1], rows.shape[0]
    wide, tall = ((size, 3 * size), bf16), ((3 * size, size), bf16)
    shapes = [((size, size), f32), ((count, size), f32), ((size, size), f32)]
    shapes = shapes + [wide, tall, wide, tall, wide, ((count, 3 * size), bf16)]
    whole = pl.BlockSpec(memory_space=pltpu.VMEM)
    return pl.pallas_call(
        chain_kernel,
        out_shape=jax.ShapeDtypeStruct(rows.shape, dtype),
        in_specs=[whole] * 2,
        out_specs=whole,
        scratch_shapes=[pltpu.VMEM(*shape) for shape in shapes],
        compiler_params=pltpu.CompilerParams(vmem_limit_bytes=56 * 1024 * 1024),
        cost_estimate=pl.CostEstimate(
            flops=6 * (13 * size + 5 * count) * size * size,
            bytes_accessed=8 * gram.size,
            transcendentals=0,
        ),
    )(gram, rows)


def body(
    query_ids,
    passage_ids,
    passage_len,
    positives,
    domains,
    table,
    table_m,
    table_v,
    pos_table,
    pos_m,
    pos_v,
    vector,
    vector_m,
    vector_v,
    w_qkv,
    m_qkv,
    w_attn,
    m_attn,
    w_in,
    m_in,
    w_out,
    m_out,
    w_proj,
    m_proj,
):
    blocks = lax.axis_size("blk")
    narrow = lax.axis_size("narrow")
    devices = blocks * narrow
    both = ("blk", "narrow")
    myself = lax.axis_index("blk")
    shard_rows = table.shape[0]
    micro_count, _, query_len = query_ids.shape
    span = passage_ids.shape[2]
    length = query_len + span
    tokens = micro_count * length

    side = D // narrow
    vector_cols = vector.shape[1] // side
    small = jnp.concatenate(
        [
            low(pos_table).T,
            low(w_proj).T,
            low(vector).reshape(side, vector_cols),
            jnp.zeros((side, D - span - VDIM - vector_cols), bf16),
        ],
        axis=1,
    )


    def gather(shard):
        return lax.all_gather(shard, "narrow", axis=0, tiled=True)


    def gather(shard):
        return lax.all_gather(shard, "narrow", axis=0, tiled=True)

    first = gather(jnp.concatenate([small, low(w_attn).T], axis=1))
    small, attn_t = first[:, :D], first[:, D:]
    qkv_t = gather(low(w_qkv).T)
    in_t = gather(low(w_in).T)
    out_t = gather(low(w_out).T)
    pos = small[:, :span].T.astype(f32)
    proj_t = small[:, span : span + VDIM]
    gains = small[:, span + VDIM : span + VDIM + vector_cols].reshape(-1).astype(f32)
    bounds = [0, D, 2 * D, 3 * D, 4 * D, 5 * D, 6 * D, 7 * D, 7 * D + FF, 8 * D + FF, 9 * D + FF]
    bounds = bounds + [10 * D + FF]
    pieces = [gains[None, bounds[index] : bounds[index + 1]] for index in range(11)]
    qkv_bias = jnp.concatenate([pieces[2], jnp.zeros_like(pieces[2]), pieces[3]], axis=1)

    slots = round_up(SLOT_CAPS.get(shard_rows, tokens), 8)
    ids = jnp.concatenate([query_ids[:, 0], passage_ids[:, 0]], axis=1).reshape(tokens)
    owner = ids // shard_rows
    local_id = ids - owner * shard_rows
    is_owner = owner[:, None] == jnp.arange(devices, dtype=jnp.int32)[None]
    before = jnp.arange(tokens)[:, None] > jnp.arange(tokens)[None]
    earlier = dot_nn(before.astype(bf16), is_owner.astype(bf16))
    rank = jnp.sum(jnp.where(is_owner, earlier, 0.0), axis=1).astype(jnp.int32)
    place = owner * slots + rank
    picks = (place[:, None] == jnp.arange(devices * slots, dtype=jnp.int32)[None]).astype(bf16)
    picks_t = (jnp.arange(devices * slots, dtype=jnp.int32)[:, None] == place[None]).astype(bf16)
    picks = lax.optimization_barrier(picks)
    digits = jnp.stack([local_id // 32, local_id % 32], axis=1).astype(bf16)
    asked = dot_tn(digits, picks)
    asked = (asked[0] * 32.0 + asked[1]).astype(jnp.int32).reshape(devices, slots)
    wanted = lax.all_to_all(asked, both, 0, 0, tiled=True).reshape(devices * slots)
    chosen = (wanted[:, None] == jnp.arange(shard_rows, dtype=jnp.int32)[None]).astype(bf16)
    chosen_t = (jnp.arange(shard_rows, dtype=jnp.int32)[:, None] == wanted[None]).astype(bf16)
    chosen = lax.optimization_barrier(chosen)
    sent_rows = low(dot_nn(chosen, low(table))).reshape(devices, slots, D)
    got_rows = lax.all_to_all(sent_rows, both, 0, 0, tiled=True).reshape(devices * slots, D)
    token_rows = dot_nn(picks, got_rows)

    per = blocks // MATRICES
    turn_of = myself // per
    wide_rows = FF // devices

    def padded(rows):
        spare = wide_rows - rows.shape[-2]
        return jnp.pad(rows, ((0, 0),) * (rows.ndim - 2) + ((0, spare), (0, 0)))

    old = [padded(member.T.reshape(blocks, -1, D)) for member in (m_qkv, m_attn, m_in, m_out)]
    old = lax.dynamic_index_in_dim(jnp.stack(old), turn_of, 0, keepdims=False).reshape(-1, D)
    token_rows, old, picks_t, chosen_t = tie(token_rows, old, picks_t, chosen_t)

    lens = passage_len[:, 0]
    pos_rows = jnp.concatenate([pos[:query_len], pos] * micro_count, axis=0)
    x, x_hat, x_scale = norm_forward(token_rows + pos_rows, pieces[0], pieces[1])
    x_low = low(x)
    qkv = low(dot_nt(x_low, qkv_t) + qkv_bias)
    context, norms = attention_forward(lens, qkv, query_len, span)
    heads = round_up(HEADS, 8)
    norms = norms.reshape(micro_count, length, 128)[:, :, :heads].transpose(0, 2, 1)
    norms = jnp.concatenate([norms[:, :, query_len:], norms[:, :, :query_len]], axis=2)
    h, h_hat, h_scale = norm_forward(
        x + dot_nt(context, attn_t) + pieces[4], pieces[5], pieces[6]
    )
    h_low = low(h)
    wide = lax.optimization_barrier(dot_nt(h_low, in_t) + pieces[7])
    gelu_value, gelu_slope = gelu_parts(wide)
    f_low, gelu_slope = tie(low(gelu_value), gelu_slope)
    o, o_hat, o_scale = norm_forward(h + dot_nn(f_low, out_t) + pieces[8], pieces[9], pieces[10])
    o_low = low(o)
    e = dot_nn(o_low, proj_t)
    e_scale = lax.rsqrt(jnp.sum(e * e, axis=-1, keepdims=True) + 1e-06)
    vecs = low(e * e_scale)

    labels = domains[:, 0]
    targets = positives[:, 0]
    spots = jnp.arange(blocks, dtype=jnp.int32)
    chosen_label = jnp.sum(
        jnp.where(targets[:, :, None] == spots[None, None], labels[:, None, :], 0), axis=-1
    )

    def spread(mask):
        mask = mask.astype(f32).transpose(1, 0, 2).reshape(blocks, micro_count * blocks, 1)
        return jnp.broadcast_to(mask, (blocks, micro_count * blocks, 128))

    allowed = spread(labels[:, :, None] == chosen_label[:, None, :])
    hits = spread(targets[:, None, :] == spots[None, :, None])
    vecs, allowed, hits = tie(vecs, allowed, hits)
    by_micro = vecs.reshape(micro_count, length, VDIM)
    cycle = by_micro[:, :query_len].reshape(micro_count * query_len, VDIM)
    cycle = share_all(cycle, "blk", blocks).reshape(blocks, micro_count * query_len, VDIM)
    share, scores = score_forward(lens, cycle, vecs, query_len, span)
    every = share_all(scores.reshape(micro_count * blocks, 128), "blk", blocks)
    every = every.reshape(blocks, micro_count * blocks, 128)
    loss_part, d_passage, d_cycle = score_backward(
        myself, every, allowed, hits, share, cycle, vecs, query_len, span
    )
    loss_part = loss_part[0, 0]
    d_query = jnp.sum(lax.all_to_all(d_cycle, "blk", 0, 0, tiled=True), axis=0)
    d_query = d_query.reshape(micro_count, query_len, VDIM)
    d_vecs = jnp.concatenate([d_query, d_passage], axis=1).reshape(tokens, VDIM)

    def reduction(pieces, wire):
        return Reduction(pieces[1::2], pieces[0::2], narrow, blocks, wire)

    def column_sum(values):
        return jnp.sum(values, axis=0)

    d_vecs = low(d_vecs).astype(f32)
    inner = jnp.sum(e * d_vecs, axis=-1, keepdims=True)
    d_e = low(e_scale * d_vecs - e * (e_scale * e_scale * e_scale * inner))
    g_proj = dot_tn(o_low, d_e)
    d_o = low(dot_nt(d_e, proj_t)).astype(f32)
    g_gain_o, g_shift_o = column_sum(d_o * o_hat), column_sum(d_o)
    d_sum_o = norm_backward(d_o, o_hat, o_scale, pieces[9])
    g_bias_out = column_sum(d_sum_o)
    d_y = low(d_sum_o)
    place = lax.axis_index("narrow")
    low_bit = place & 1
    g_out = dot_tn(f_low, d_y).reshape(narrow // 2, 2, -1, D)
    out_sent = lax.dynamic_index_in_dim(g_out, 1 - low_bit, 1, keepdims=False)
    d_y, out_sent, g_out = tie(d_y, out_sent, g_out)
    out_got = swap(out_sent, "narrow", narrow, 1)
    d_f = low(dot_nt(d_y, out_t)).astype(f32)
    d_wide = d_f * gelu_slope
    g_bias_in = column_sum(d_wide)
    d_wide = low(d_wide)
    d_wide, out_got = tie(d_wide, out_got)
    g_out = lax.dynamic_index_in_dim(g_out, low_bit, 1, keepdims=False) + out_got
    g_out = low(g_out.reshape(-1, D))
    d_wide, g_out = tie(d_wide, g_out)
    if narrow > 2:
        groups = [list(range(bit, narrow, 2)) for bit in range(2)]
        g_out = lax.psum_scatter(
            g_out, "narrow", scatter_dimension=0, axis_index_groups=groups, tiled=True
        )
    sum_in = reduction(relative(dot_tn(d_wide, h_low), narrow), bf16)
    d_wide, sum_in.sent = tie(d_wide, sum_in.sent)
    sum_in.across_core()
    d_wide, sum_in.kept = tie(d_wide, sum_in.kept)
    sum_in.prepare()
    d_wide, sum_in.outgoing, sum_in.kept = tie(d_wide, sum_in.outgoing, sum_in.kept)
    sum_in.send()
    d_h = d_sum_o + low(dot_nn(d_wide, in_t)).astype(f32)
    g_gain_h, g_shift_h = column_sum(d_h * h_hat), column_sum(d_h)
    d_sum_h = norm_backward(d_h, h_hat, h_scale, pieces[5])
    g_bias_attn = column_sum(d_sum_h)
    d_a = low(d_sum_h)
    sum_attn = reduction(relative(dot_tn(d_a, context), narrow), bf16)
    d_a, sum_attn.sent, g_out = tie(d_a, sum_attn.sent, g_out)
    g_out = lax.psum_scatter(g_out.astype(f32), "blk", scatter_dimension=0, tiled=True)
    sum_attn.across_core()
    d_context = low(dot_nn(d_a, attn_t))
    d_context, sum_attn.got = tie(d_context, sum_attn.got)
    sum_attn.across_narrow()
    head_of = jnp.arange(D)[None] // HDIM == jnp.arange(heads)[:, None]
    inner = lax.dot_general(
        head_of.astype(f32),
        d_context.astype(f32) * context.astype(f32),
        (((1,), (1,)), ((), ())),
        precision=lax.Precision.HIGH,
        preferred_element_type=f32,
    )
    inner = inner.reshape(heads, micro_count, length).transpose(1, 0, 2)
    inner = jnp.concatenate([inner[:, :, query_len:], inner[:, :, :query_len]], axis=2)
    d_qkv = attention_backward(lens, qkv, d_context, norms, inner, query_len, span)
    d_qkv, sum_in.got, sum_attn.got = tie(d_qkv, sum_in.got, sum_attn.got)
    g_in = sum_in.total()
    d_qkv, g_in = tie(d_qkv, g_in)
    g_in = lax.psum_scatter(g_in, "blk", scatter_dimension=0, tiled=True)
    d_x = d_sum_h + low(dot_nn(d_qkv, qkv_t)).astype(f32)
    d_rows = norm_backward(d_x, x_hat, x_scale, pieces[0])

    back_rows = low(dot_nn(picks_t, low(d_rows))).reshape(devices, slots, D)
    back_rows, d_rows, d_x, d_qkv, g_proj = tie(back_rows, d_rows, d_x, d_qkv, g_proj)
    back_rows = lax.all_to_all(back_rows, both, 0, 0, tiled=True).reshape(devices * slots, D)
    sum_qkv = reduction(relative(dot_tn(d_qkv, x_low), narrow), bf16)
    d_qkv, d_rows, d_x, sum_qkv.sent = tie(d_qkv, d_rows, d_x, sum_qkv.sent)
    sum_qkv.across_core()
    sum_qkv.across_narrow()
    early = (g_bias_attn, g_gain_h, g_shift_h, g_bias_in, g_bias_out, g_gain_o, g_shift_o)
    tail = late_sums(d_rows, d_x, x_hat, d_qkv, g_proj, early, query_len, span, micro_count)
    sum_tail = reduction(relative(tail, narrow), f32)
    sum_tail.across_core()
    sum_tail.across_narrow()
    tail = sum_tail.total()
    spare_high = lax.optimization_barrier(low(tail[:, span:]))
    tail = [low(tail[:, :span]), spare_high, low(tail[:, span:] - spare_high.astype(f32))]
    tail = jnp.concatenate(tail, axis=1).reshape(blocks, -1)
    tail_size = tail.shape[1]
    tail = jnp.pad(tail, ((0, 0), (0, round_up(tail_size, 16 * D) - tail_size)))
    merged = [low(member.total()).reshape(blocks, -1, D) for member in (sum_qkv, sum_attn)]
    merged = jnp.concatenate(merged + [tail.reshape(blocks, -1, D)], axis=1)
    merged, back_rows = tie(merged, back_rows)
    merged = lax.all_to_all(merged, "blk", 0, 0, tiled=True)
    table_grad = dot_nn(chosen_t, back_rows)
    table_square = jnp.sum(table_grad * table_grad)
    merged = jnp.sum(merged.astype(f32), axis=0)
    attn_rows = D // devices
    qkv_rows = 3 * attn_rows
    g_qkv, g_attn = merged[:qkv_rows], merged[qkv_rows : qkv_rows + attn_rows]
    g_tail = merged[qkv_rows + attn_rows :].reshape(-1)[:tail_size].reshape(attn_rows, -1)
    spare = g_tail[:, span : span + 128 + VDIM] + g_tail[:, span + 128 + VDIM :]
    g_tail = jnp.concatenate([g_tail[:, :span], spare], axis=1)
    g_qkv, g_attn, g_out, g_in, g_tail, table_square = tie(
        g_qkv, g_attn, g_out, g_in, g_tail, table_square
    )

    sends = [padded(low(member)) for member in (g_qkv, g_attn, g_in, g_out)]
    sends = jnp.repeat(jnp.stack(sends), per, axis=0)
    taken = lax.all_to_all(sends, "blk", 0, 0, tiled=True)

    def square_sum(values):
        values = values.astype(f32)
        return jnp.sum(values * values)

    local_square = (
        table_square
        + square_sum(g_out)
        + square_sum(g_in)
        + square_sum(g_qkv)
        + square_sum(g_attn)
        + square_sum(g_tail)
    )
    lane = lax.broadcasted_iota(jnp.int32, (8, 128), 1)
    pair = jnp.where(lane == 0, local_square, jnp.where(lane == 1, loss_part, 0.0))
    sums = sum_everywhere(pair, (("narrow", narrow), ("blk", blocks)))
    loss = sums[0, 1]
    grad_norm = jnp.sqrt(sums[0, 0])
    factor = jnp.minimum(1.0, clip_limit / (grad_norm + 1e-06))

    packed = [low(member) for member in (g_qkv, g_attn, g_in, g_out, g_tail)]
    complete = lax.all_gather(jnp.concatenate(packed, axis=0), "blk", axis=0, tiled=False)
    moment, gram = packed_gram(factor, old, taken.reshape(-1, D))
    gram = sum_group(gram, narrow, 1, blocks)
    half = moment.shape[0] // per
    moment = lax.dynamic_slice_in_dim(moment, myself % per * half, half, axis=0)
    ortho = newton_chain(gram, moment, bf16)
    ortho, complete = tie(ortho, complete)
    ortho = lax.all_gather(ortho, "blk", axis=0, tiled=False)
    ortho = ortho.reshape(MATRICES, blocks, wide_rows, D)
    matrix_rows = (qkv_rows, attn_rows, wide_rows, wide_rows)

    def turned(rows):
        return rows.reshape(-1, D).T.astype(f32)

    grads, first = [], 0
    for rows in matrix_rows:
        grads.append(turned(complete[:, first : first + rows]))
        first += rows
    tail_all = complete[:, first:].reshape(side, -1)
    grad_pos = tail_all[:, :span].T.astype(f32)
    grad_proj = tail_all[:, span + 128 :].T.astype(f32)
    grad_vector = tail_all[:, span : span + 128].T
    grad_bias = grad_vector[4:5].astype(f32)
    place = lax.axis_index("narrow")
    whole_vector = jnp.zeros((narrow,) + grad_vector.shape, bf16)
    for offset, piece in enumerate(gather_relative(grad_vector, narrow)):
        whole_vector = lax.dynamic_update_index_in_dim(whole_vector, piece, place ^ offset, 0)
    whole_vector = whole_vector.transpose(1, 0, 2)[:vector_cols].reshape(1, -1).astype(f32)
    grad_vector = lax.dynamic_slice_in_dim(
        whole_vector, place * vector.shape[1], vector.shape[1], axis=1
    )
    proj_rows, gram_proj = packed_gram(factor, m_proj.T, grad_proj.T)
    ortho_proj = newton_chain(sum_group(gram_proj, narrow, 1, blocks), proj_rows, f32)
    table_new, table_m_new, table_v_new = adam_step(
        table, table_m, table_v, factor * table_grad, adam_rate
    )
    pos_new, pos_m_new, pos_v_new = adam_step(
        pos_table, pos_m, pos_v, factor * grad_pos, adam_rate
    )
    vector_new, vector_m_new, vector_v_new = adam_step(
        vector, vector_m, vector_v, factor * grad_vector, vector_rate
    )
    olds = (m_qkv, m_attn, m_in, m_out, m_proj)
    grads = grads + [grad_proj]
    moments = [muon_moment * before + factor * grad for before, grad in zip(olds, grads)]
    masters = (w_qkv, w_attn, w_proj)
    orthos = (turned(ortho[0, :, :qkv_rows]), turned(ortho[1, :, :attn_rows]), ortho_proj.T)
    updated = []
    for weight, ortho_part, rate in zip(masters, orthos, (muon_rate, attn_rate, muon_rate)):
        long_side = max(weight.shape[0], weight.shape[1] * narrow)
        updated.append(weight - rate * (0.2 * long_side**0.5 * ortho_part + weight_decay * weight))
    wide_orthos = [ortho[index].reshape(-1, D) for index in (2, 3)]
    in_new, out_new = update_wide((w_in, w_out), wide_orthos, muon_rate, 0.2 * FF**0.5)
    updated = [updated[0], updated[1], in_new, out_new, updated[2]]
    return (
        loss,
        grad_norm,
        table_new,
        table_m_new,
        table_v_new,
        pos_new,
        pos_m_new,
        pos_v_new,
        vector_new,
        vector_m_new,
        vector_v_new,
        updated[0],
        moments[0],
        updated[1],
        moments[1],
        updated[2],
        moments[2],
        updated[3],
        moments[3],
        updated[4],
        moments[4],
        factor * grad_bias,
    )


def solution(mesh):
    ids = P(None, ("blk", "narrow"), None)
    rows = P(("blk", "narrow"), None)
    cols = P(None, "narrow")
    group = P(None, "narrow", None)
    in_specs = (ids, ids, P(None, ("blk", "narrow")), group, group) + (rows,) * 3 + (cols,) * 16
    out_specs = (P(), P()) + (rows,) * 3 + (cols,) * 17
    return jax.shard_map(body, mesh=mesh, in_specs=in_specs, out_specs=out_specs, check_vma=False)
```

```python
import functools

import jax
import jax.numpy as jnp
from jax import lax
from jax.experimental import pallas as pl
from jax.experimental.pallas import tpu as pltpu
from jax.sharding import PartitionSpec as P

D = 768
HEADS = 12
HDIM = 64
FF = 3072
VDIM = 128
STEP = 10
MATRICES = 4

norm_eps = 1e-12
smoothing = 0.1
masked = -1e30
newton_one = 3.4445
newton_two = -4.775
newton_three = 2.0315
muon_rate = 0.1
attn_rate = 1.0
muon_moment = 0.95
weight_decay = 0.01
adam_rate = 0.02
vector_rate = 0.25
beta_one = 0.9
beta_two = 0.95
adam_eps = 1e-08
clip_limit = 0.05

bf16 = jnp.bfloat16
f32 = jnp.float32
SLOT_CAPS = {960: 36, 120: 7}


def round_up(value, step):
    return -(-value // step) * step


def dot_nn(left, right):
    return lax.dot_general(left, right, (((1,), (0,)), ((), ())), preferred_element_type=f32)


def dot_nt(left, right):
    return lax.dot_general(left, right, (((1,), (1,)), ((), ())), preferred_element_type=f32)


def dot_tn(left, right):
    return lax.dot_general(left, right, (((0,), (0,)), ((), ())), preferred_element_type=f32)


def low(values):
    return values.astype(bf16)


def norm_forward(values, gain, shift):
    centred = values - jnp.mean(values, axis=-1, keepdims=True)
    spread = jnp.mean(centred * centred, axis=-1, keepdims=True)
    scale = lax.rsqrt(spread + norm_eps)
    hat = centred * scale
    return hat * gain + shift, hat, scale


def norm_backward(grad, hat, scale, gain):
    d_hat = grad * gain
    first = jnp.mean(d_hat, axis=-1, keepdims=True)
    second = jnp.mean(d_hat * hat, axis=-1, keepdims=True)
    return scale * (d_hat - first - hat * second)


def gelu_parts(values):
    cdf = 0.5 * (1.0 + lax.erf(values * (0.5**0.5)))
    density = jnp.exp(-0.5 * values * values) * 0.3989422804014327
    return values * cdf, cdf + values * density


def attention_forward_kernel(
    lens_ref, qkv_ref, out_ref, norm_ref, scores_one, scores_two, share_one, share_two, *, query_len, span
):
    used = lens_ref[pl.program_id(0)]
    bias_long = jnp.where(lax.broadcasted_iota(jnp.int32, (1, span), 1) < used, 0.0, masked)
    bias_short = jnp.zeros((1, query_len), f32)
    lane_of = lax.broadcasted_iota(jnp.int32, (16, 128), 1)
    norm_ref[...] = jnp.zeros_like(norm_ref)

    def attend(first, count, lane, half, bias, head, scores_ref, share_ref):
        rows, span_of = pl.ds(first, count), pl.ds(0, count)
        queries = qkv_ref[rows, pl.ds(lane, 128)][:, half] * bf16(HDIM**-0.5)
        keys = qkv_ref[rows, pl.ds(lane + D, 128)][:, half]
        values = qkv_ref[rows, pl.ds(lane + 2 * D, 128)][:, half]
        scores_ref[span_of, span_of] = dot_nt(queries, keys)
        for step in range(0, count, 16):
            here = pl.ds(step, 16)
            scores = scores_ref[here, span_of] + bias
            peak = jnp.max(scores, axis=-1, keepdims=True)
            exponent = jnp.exp(scores - peak)
            total = jnp.sum(exponent, axis=-1, keepdims=True)
            share_ref[here, span_of] = low(exponent * (1.0 / total))
            there = pl.ds(first + step, 16)
            norm_ref[there, :] = jnp.where(lane_of == head, peak + jnp.log(total), norm_ref[there, :])
        return dot_nn(share_ref[span_of, span_of], values)

    def pair(index, carry):
        lane = pl.multiple_of(index * 128, 128)
        for first, count, bias in ((0, query_len, bias_short), (query_len, span, bias_long)):
            one = attend(
                first, count, lane, slice(0, HDIM), bias, 2 * index, scores_one, share_one
            )
            two = attend(
                first, count, lane, slice(HDIM, 128), bias, 2 * index + 1, scores_two, share_two
            )
            out_ref[pl.ds(first, count), pl.ds(lane, 128)] = low(jnp.concatenate([one, two], axis=1))
        return carry

    lax.fori_loop(0, HEADS // 2, pair, 0)


def attention_forward(lens, qkv, query_len, span):
    length = query_len + span
    tokens = qkv.shape[0]
    micro_count = tokens // length
    block = pl.BlockSpec((length, 3 * D), lambda micro, lens: (micro, 0))
    square = [pltpu.VMEM((span, span), f32)] * 2 + [pltpu.VMEM((span, span), bf16)] * 2
    return pl.pallas_call(
        functools.partial(attention_forward_kernel, query_len=query_len, span=span),
        out_shape=(
            jax.ShapeDtypeStruct((tokens, D), bf16),
            jax.ShapeDtypeStruct((tokens, 128), f32),
        ),
        grid_spec=pltpu.PrefetchScalarGridSpec(
            num_scalar_prefetch=1,
            grid=(micro_count,),
            in_specs=[block],
            out_specs=(
                pl.BlockSpec((length, D), lambda micro, lens: (micro, 0)),
                pl.BlockSpec((length, 128), lambda micro, lens: (micro, 0)),
            ),
            scratch_shapes=square,
        ),
        compiler_params=pltpu.CompilerParams(vmem_limit_bytes=48 * 1024 * 1024),
        cost_estimate=pl.CostEstimate(
            flops=8 * micro_count * HEADS * span * span * HDIM,
            bytes_accessed=tokens * 8 * D,
            transcendentals=micro_count * HEADS * span * span,
        ),
    )(lens, qkv)


def attention_backward_kernel(
    lens_ref,
    qkv_ref,
    grad_ref,
    norm_ref,
    inner_ref,
    out_ref,
    scores_one,
    scores_two,
    slopes_one,
    slopes_two,
    share_one,
    share_two,
    d_one,
    d_two,
    *,
    query_len,
    span,
):
    used = lens_ref[pl.program_id(0)]
    bias_long = jnp.where(lax.broadcasted_iota(jnp.int32, (span, 1), 0) < used, 0.0, masked)
    bias_short = jnp.zeros((query_len, 1), f32)

    def attend(first, count, lane, half, bias, head, scores_ref, slopes_ref, share_ref, d_ref):
        rows, span_of = pl.ds(first, count), pl.ds(0, count)
        queries = qkv_ref[rows, pl.ds(lane, 128)][:, half] * bf16(HDIM**-0.5)
        keys = qkv_ref[rows, pl.ds(lane + D, 128)][:, half]
        values = qkv_ref[rows, pl.ds(lane + 2 * D, 128)][:, half]
        grads = grad_ref[rows, pl.ds(lane, 128)][:, half]
        lanes = slice(0, count) if first else slice(span, span + count)
        norm = norm_ref[0, pl.ds(head, 1), :][:, lanes]
        inner = inner_ref[0, pl.ds(head, 1), :][:, lanes]
        scores_ref[span_of, span_of] = dot_nt(keys, queries)
        slopes_ref[span_of, span_of] = dot_nt(values, grads)
        for step in range(0, count, 16):
            here = pl.ds(step, 16)
            scores = scores_ref[here, span_of] + bias[step : step + 16]
            share = jnp.exp(scores - norm)
            share_ref[here, span_of] = low(share)
            d_ref[here, span_of] = low(share * (slopes_ref[here, span_of] - inner))
        d_scores = d_ref[span_of, span_of]
        d_values = dot_nn(share_ref[span_of, span_of], grads)
        d_keys = dot_nn(d_scores, queries)
        d_queries = dot_tn(d_scores, keys) * HDIM**-0.5
        return d_queries, d_keys, d_values

    def pair(index, carry):
        lane = pl.multiple_of(index * 128, 128)
        for first, count, bias in ((0, query_len, bias_short), (query_len, span, bias_long)):
            one = attend(
                first,
                count,
                lane,
                slice(0, HDIM),
                bias,
                2 * index,
                scores_one,
                slopes_one,
                share_one,
                d_one,
            )
            two = attend(
                first,
                count,
                lane,
                slice(HDIM, 128),
                bias,
                2 * index + 1,
                scores_two,
                slopes_two,
                share_two,
                d_two,
            )
            for part in range(3):
                both = jnp.concatenate([one[part], two[part]], axis=1)
                out_ref[pl.ds(first, count), pl.ds(lane + part * D, 128)] = low(both)
        return carry

    lax.fori_loop(0, HEADS // 2, pair, 0)


def attention_backward(lens, qkv, grad, norm, inner, query_len, span):
    length = query_len + span
    tokens = qkv.shape[0]
    micro_count = tokens // length
    heads = norm.shape[1]

    def block(width):
        return pl.BlockSpec((length, width), lambda micro, lens: (micro, 0))

    row = pl.BlockSpec((1, heads, length), lambda micro, lens: (micro, 0, 0))
    square = [pltpu.VMEM((span, span), f32)] * 4 + [pltpu.VMEM((span, span), bf16)] * 4
    return pl.pallas_call(
        functools.partial(attention_backward_kernel, query_len=query_len, span=span),
        out_shape=jax.ShapeDtypeStruct((tokens, 3 * D), bf16),
        grid_spec=pltpu.PrefetchScalarGridSpec(
            num_scalar_prefetch=1,
            grid=(micro_count,),
            in_specs=[block(3 * D), block(D), row, row],
            out_specs=block(3 * D),
            scratch_shapes=square,
        ),
        compiler_params=pltpu.CompilerParams(vmem_limit_bytes=48 * 1024 * 1024),
        cost_estimate=pl.CostEstimate(
            flops=20 * micro_count * HEADS * span * span * HDIM,
            bytes_accessed=tokens * 14 * D,
            transcendentals=micro_count * HEADS * span * span,
        ),
    )(lens, qkv, grad, norm, inner)


def update_kernel(*refs, rate, scale):
    count = len(refs) // 3
    for weight, ortho, out in zip(refs[:count], refs[count : 2 * count], refs[2 * count :]):
        turned = ortho[...].astype(f32).T
        out[...] = weight[...] - rate * (scale * turned + weight_decay * weight[...])


def update_wide(weights, orthos, rate, scale):
    rows, columns = weights[0].shape
    step = 128
    weight_spec = pl.BlockSpec((rows, step), lambda place: (0, place))
    ortho_spec = pl.BlockSpec((step, rows), lambda place: (place, 0))
    count = len(weights)
    return pl.pallas_call(
        functools.partial(update_kernel, rate=rate, scale=scale),
        grid=(columns // step,),
        in_specs=[weight_spec] * count + [ortho_spec] * count,
        out_specs=(weight_spec,) * count,
        out_shape=(jax.ShapeDtypeStruct((rows, columns), f32),) * count,
        compiler_params=pltpu.CompilerParams(vmem_limit_bytes=32 * 1024 * 1024),
        cost_estimate=pl.CostEstimate(
            flops=4 * count * rows * columns,
            bytes_accessed=10 * count * rows * columns,
            transcendentals=0,
        ),
    )(*weights, *orthos)


def score_kernel(lens_ref, cycle_ref, vecs_ref, share_ref, scores_ref, *, query_len, span):
    micro = pl.program_id(0)
    blocks = cycle_ref.shape[0]
    mine = pl.ds(pl.multiple_of(micro * query_len, query_len), query_len)
    queries = jnp.concatenate([cycle_ref[place, mine, :] for place in range(blocks)], axis=0)
    first = pl.multiple_of(micro * (query_len + span) + query_len, query_len)
    sims = dot_nt(queries, vecs_ref[pl.ds(first, span), :])
    used = lax.broadcasted_iota(jnp.int32, (1, span), 1) < lens_ref[micro]
    scaled = jnp.where(used, sims / smoothing, masked)
    summit = jnp.max(scaled, axis=-1, keepdims=True)
    exponent = jnp.exp(scaled - summit)
    total = jnp.sum(exponent, axis=-1, keepdims=True)
    share_ref[0] = exponent / total
    smooth = smoothing * (summit + jnp.log(total))
    smooth = jnp.broadcast_to(smooth, (blocks * query_len, 128))
    scores_ref[0] = jnp.sum(smooth.reshape(blocks, query_len, 128), axis=1)


def score_forward(lens, cycle, vecs, query_len, span):
    blocks, micro_count = cycle.shape[0], lens.shape[0]
    rows = blocks * query_len
    return pl.pallas_call(
        functools.partial(score_kernel, query_len=query_len, span=span),
        out_shape=(
            jax.ShapeDtypeStruct((micro_count, rows, span), f32),
            jax.ShapeDtypeStruct((micro_count, blocks, 128), f32),
        ),
        grid_spec=pltpu.PrefetchScalarGridSpec(
            num_scalar_prefetch=1,
            grid=(micro_count,),
            in_specs=[
                pl.BlockSpec(cycle.shape, lambda micro, lens: (0, 0, 0)),
                pl.BlockSpec(vecs.shape, lambda micro, lens: (0, 0)),
            ],
            out_specs=(
                pl.BlockSpec((1, rows, span), lambda micro, lens: (micro, 0, 0)),
                pl.BlockSpec((1, blocks, 128), lambda micro, lens: (micro, 0, 0)),
            ),
        ),
        compiler_params=pltpu.CompilerParams(vmem_limit_bytes=48 * 1024 * 1024),
        cost_estimate=pl.CostEstimate(
            flops=2 * micro_count * rows * span * VDIM,
            bytes_accessed=4 * micro_count * rows * span,
            transcendentals=micro_count * rows * span,
        ),
    )(lens, cycle, vecs)


def loss_kernel(
    me_ref,
    every_ref,
    allowed_ref,
    hits_ref,
    share_ref,
    cycle_ref,
    vecs_ref,
    loss_ref,
    passage_ref,
    query_ref,
    *,
    query_len,
    span,
):
    me = me_ref[0]
    blocks = cycle_ref.shape[0]
    micro_count = share_ref.shape[0]
    every = every_ref[...]
    allowed = allowed_ref[...] > 0.0
    peak = jnp.max(jnp.where(allowed, every, masked), axis=0)
    mass = jnp.sum(jnp.where(allowed, jnp.exp(every - peak[None]), 0.0), axis=0)
    log_total = peak + jnp.log(mass)
    matched = jnp.sum(jnp.where(hits_ref[...] > 0.0, every, 0.0), axis=0)
    row = lax.broadcasted_iota(jnp.int32, log_total.shape, 0)
    mine = jnp.where(row % blocks == me, log_total - matched, 0.0)
    loss_ref[...] = jnp.broadcast_to(jnp.sum(mine, axis=0, keepdims=True), loss_ref.shape)
    d_scores = jnp.where(allowed_ref[me] > 0.0, jnp.exp(every_ref[me] - log_total), 0.0)
    d_scores = d_scores - hits_ref[me]
    for micro in range(micro_count):
        own = d_scores[micro * blocks : (micro + 1) * blocks]
        own = jnp.broadcast_to(own[:, None, :], (blocks, query_len, 128))
        own = own.reshape(blocks * query_len, 128)[:, 0:1]
        d_sims = low(own * share_ref[micro])
        here = slice(micro * query_len, (micro + 1) * query_len)
        queries = jnp.concatenate([cycle_ref[place, here, :] for place in range(blocks)], axis=0)
        first = micro * (query_len + span) + query_len
        passage_ref[micro] = dot_tn(d_sims, queries)
        d_queries = dot_nn(d_sims, vecs_ref[first : first + span, :])
        for place in range(blocks):
            rows = slice(place * query_len, (place + 1) * query_len)
            query_ref[place, here, :] = d_queries[rows]


def score_backward(me, every, allowed, hits, share, cycle, vecs, query_len, span):
    micro_count = share.shape[0]
    whole = pl.BlockSpec(memory_space=pltpu.VMEM)
    return pl.pallas_call(
        functools.partial(loss_kernel, query_len=query_len, span=span),
        out_shape=(
            jax.ShapeDtypeStruct((8, 128), f32),
            jax.ShapeDtypeStruct((micro_count, span, VDIM), f32),
            jax.ShapeDtypeStruct(cycle.shape, f32),
        ),
        in_specs=[pl.BlockSpec(memory_space=pltpu.SMEM)] + [whole] * 6,
        out_specs=(whole,) * 3,
        compiler_params=pltpu.CompilerParams(vmem_limit_bytes=48 * 1024 * 1024),
        cost_estimate=pl.CostEstimate(
            flops=4 * share.size * VDIM, bytes_accessed=4 * share.size, transcendentals=0
        ),
    )(me.reshape(1).astype(jnp.int32), every, allowed, hits, share, cycle, vecs)


def tail_kernel(rows_ref, x_ref, hat_ref, qkv_ref, proj_ref, *refs, query_len, span, micro_count):
    out_ref = refs[-1]
    length = query_len + span
    for first in range(0, span, 128):
        block = rows_ref[query_len + first : query_len + first + 128, :]
        for micro in range(1, micro_count):
            start = micro * length + query_len + first
            block = block + rows_ref[start : start + 128, :]
        if first == 0:
            head = rows_ref[0:query_len, :]
            for micro in range(1, micro_count):
                head = head + rows_ref[micro * length : micro * length + query_len, :]
            block = jnp.concatenate([block[:query_len] + head, block[query_len:]], axis=0)
        out_ref[:, first : first + 128] = block.T

    def fold(values):
        return jnp.sum(values.reshape(-1, 8, D), axis=0)

    sums = [jnp.zeros((8, D), f32)] * 4
    for first in range(0, micro_count * length, 32):
        here = pl.ds(first, 32)
        d_x = x_ref[here, :]
        terms = (
            d_x * hat_ref[here, :],
            d_x,
            qkv_ref[here, 0:D].astype(f32),
            qkv_ref[here, 2 * D : 3 * D].astype(f32),
        )
        sums = [total + fold(term) for total, term in zip(sums, terms)]
    sums = [jnp.sum(total, axis=0, keepdims=True) for total in sums]
    for ref in refs[:-1]:
        sums = sums + [ref[:, first : first + D] for first in range(0, ref.shape[1], D)]
    sums.append(jnp.zeros((128 - len(sums), D), f32))
    out_ref[:, span : span + 128] = jnp.concatenate(sums, axis=0).T
    out_ref[:, span + 128 :] = proj_ref[...]


def late_sums(d_rows, d_x, x_hat, d_qkv, g_proj, early, query_len, span, micro_count):
    early = [member.reshape(1, -1) for member in early]
    whole = pl.BlockSpec(memory_space=pltpu.VMEM)
    return pl.pallas_call(
        functools.partial(
            tail_kernel, query_len=query_len, span=span, micro_count=micro_count
        ),
        out_shape=jax.ShapeDtypeStruct((D, span + 128 + VDIM), f32),
        in_specs=[whole] * (5 + len(early)),
        out_specs=whole,
        compiler_params=pltpu.CompilerParams(vmem_limit_bytes=48 * 1024 * 1024),
        cost_estimate=pl.CostEstimate(
            flops=8 * d_rows.size, bytes_accessed=20 * d_rows.size, transcendentals=0
        ),
    )(d_rows, d_x, x_hat, d_qkv, g_proj, *early)


def share_all(value, axes, count):
    spread = jnp.broadcast_to(value[None], (count,) + value.shape)
    return lax.all_to_all(spread, axes, 0, 0, tiled=True)


def swap(value, axis, size, bit):
    return lax.ppermute(value, axis, [(place, place ^ bit) for place in range(size)])


def gather_relative(shard, narrow):
    pieces = {0: shard}
    bit = narrow // 2
    while bit:
        for offset in list(pieces):
            pieces[offset ^ bit] = swap(pieces[offset], "narrow", narrow, bit)
        bit = bit // 2
    return [pieces[offset] for offset in range(narrow)]


def relative(whole, narrow):
    place = lax.axis_index("narrow")
    rows = whole.shape[0] // narrow
    return [
        lax.dynamic_slice_in_dim(whole, (place ^ offset) * rows, rows, axis=0)
        for offset in range(narrow)
    ]


def gram_kernel(factor_ref, old_ref, grad_ref, moment_ref, gram_ref):
    moment = muon_moment * old_ref[...] + factor_ref[0] * grad_ref[...].astype(f32)
    moment_ref[...] = moment
    high, rest = split(moment)
    size = moment.shape[1]
    side = size if gram_ref.shape[0] == size else size // 3

    def part(row):
        left = slice(row, row + side)
        right = slice(row, size)
        return (
            dot_tn(high[:, left], high[:, right])
            + dot_tn(high[:, left], rest[:, right])
            + dot_tn(rest[:, left], high[:, right])
        )

    gram_ref[0:side, :] = part(0)
    if side < size:
        gram_ref[side : 2 * side, 0 : 2 * side] = part(side)
        gram_ref[side : 2 * side, 2 * side : size] = part(2 * side)


def packed_gram(factor, old, grad):
    count, size = old.shape
    whole = pl.BlockSpec(memory_space=pltpu.VMEM)
    packed = size if size < 3 * 128 else 2 * size // 3
    return pl.pallas_call(
        gram_kernel,
        out_shape=(
            jax.ShapeDtypeStruct((count, size), f32),
            jax.ShapeDtypeStruct((packed, size), f32),
        ),
        in_specs=[pl.BlockSpec(memory_space=pltpu.SMEM), whole, whole],
        out_specs=(whole, whole),
        compiler_params=pltpu.CompilerParams(vmem_limit_bytes=48 * 1024 * 1024),
        cost_estimate=pl.CostEstimate(
            flops=4 * count * size * size, bytes_accessed=14 * count * size, transcendentals=0
        ),
    )(factor.reshape(1), old, grad)


def tie(*values):
    return lax.optimization_barrier(values)


class Reduction:
    def __init__(self, sent, kept, narrow, blocks, wire):
        self.narrow, self.blocks, self.wire = narrow, blocks, wire
        self.sent, self.kept = list(sent), list(kept)

    def across_core(self):
        self.got = [swap(member, "narrow", self.narrow, 1) for member in self.sent]

    def prepare(self):
        totals = [kept + got for kept, got in zip(self.kept, self.got)]
        half = len(totals) // 2
        while half > 1:
            for offset in range(half):
                got = swap(totals[offset + half].astype(self.wire), "narrow", self.narrow, 2 * half)
                totals[offset] = totals[offset] + got.astype(f32)
            half = half // 2
        self.kept = totals[0]
        self.outgoing = totals[-1].astype(self.wire)

    def across_narrow(self):
        self.prepare()
        self.send()

    def send(self):
        if self.narrow > 2:
            self.got = swap(self.outgoing, "narrow", self.narrow, 2)
        else:
            self.got = jnp.zeros_like(self.outgoing)

    def total(self):
        return self.kept + self.got.astype(f32)


def sum_everywhere(value, sizes):
    for axis, size in sizes:
        if size <= 8:
            swaps = [swap(value, axis, size, offset) for offset in range(1, size)]
            value = sum(swaps, value)
            continue
        bit = 1
        while bit < size:
            value = value + swap(value, axis, size, bit)
            bit = bit * 2
    return value


def sum_group(value, narrow, per, blocks):
    steps = [("narrow", narrow, 1)]
    steps = steps + [("blk", blocks, 1 << bit) for bit in range(per.bit_length() - 1)]
    for axis, size, bit in steps:
        halves = value.reshape(2, value.shape[0] // 2, value.shape[1])
        mine = (lax.axis_index(axis) // bit) & 1
        sent = lax.dynamic_index_in_dim(halves, 1 - mine, 0, keepdims=False)
        got = swap(sent, axis, size, bit)
        value = lax.dynamic_index_in_dim(halves, mine, 0, keepdims=False) + got
    bit = 2
    while bit < narrow:
        value = value + swap(value, "narrow", narrow, bit)
        bit = bit * 2
    for axis, size, bit in reversed(steps):
        other = swap(value, axis, size, bit)
        lower = (lax.axis_index(axis) // bit) & 1 == 0
        value = jnp.concatenate(
            [jnp.where(lower, value, other), jnp.where(lower, other, value)], axis=0
        )
    return value


def adam_step(weight, first, second, gradient, rate):
    first_new = beta_one * first + (1.0 - beta_one) * gradient
    second_new = beta_two * second + (1.0 - beta_two) * gradient * gradient
    update = (
        first_new
        / (1.0 - beta_one**STEP)
        / (jnp.sqrt(second_new / (1.0 - beta_two**STEP)) + adam_eps)
    )
    return (weight - rate * (update + weight_decay * weight), first_new, second_new)


def split(value):
    high = low(value)
    return high, low(value - high.astype(f32))


def chain_kernel(
    gram_in, rows_in, out, gram, rows, half, gram_l, gram_r, poly_l, poly_r, half_l, rows_l
):
    size, count = gram.shape[0], rows.shape[0]
    parts = 3 if gram_in.shape[0] < size else 1
    side = size // parts

    def put(left_ref, right_ref, value, row, column):
        for piece, first, second in ((value, row, column), (value.T, column, row)):
            high, rest = split(piece)
            width = piece.shape[1]
            if left_ref is not None:
                here = pl.ds(first, piece.shape[0])
                left_ref[here, pl.ds(second, width)] = high
                left_ref[here, pl.ds(size + second, width)] = high
                left_ref[here, pl.ds(2 * size + second, width)] = rest
            if right_ref is not None:
                there = pl.ds(second, width)
                right_ref[pl.ds(first, piece.shape[0]), there] = high
                right_ref[pl.ds(size + first, piece.shape[0]), there] = rest
                right_ref[pl.ds(2 * size + first, piece.shape[0]), there] = high
            if row == column:
                break

    def store(left_ref, right_ref, value, row):
        for place in range(row // side, parts):
            column = place * side
            put(left_ref, right_ref, value[:, column - row : column - row + side], row, column)

    def put_rows(value, first):
        high, rest = split(value)
        here = pl.ds(first, value.shape[0])
        rows_l[here, 0:size] = high
        rows_l[here, size : 2 * size] = high
        rows_l[here, 2 * size : 3 * size] = rest

    def packed(row):
        if parts == 1 or row == 0:
            return gram_in[0:side, :]
        if row == side:
            return gram_in[side : 2 * side, 0 : 2 * side]
        return gram_in[side : 2 * side, 2 * side : size]

    starts = [place * side for place in range(parts)]
    row_steps = [(first, min(256, count - first)) for first in range(0, count, 256)]
    diagonal = lax.broadcasted_iota(jnp.int32, (side, side), 0) == lax.broadcasted_iota(
        jnp.int32, (side, side), 1
    )
    trace = jnp.zeros((1, 1), f32)
    for row in starts:
        block = packed(row)[:, 0:side]
        trace = trace + jnp.sum(jnp.where(diagonal, block, 0.0), axis=(0, 1), keepdims=True)
    scale = 1.0 / (jnp.sqrt(trace) + 1e-07)
    for row in starts:
        block = packed(row) * (scale * scale)
        gram[pl.ds(row, side), pl.ds(row, size - row)] = block
        store(gram_l, gram_r, block, row)
    for first, step in row_steps:
        block = rows_in[pl.ds(first, step), :] * scale
        rows[pl.ds(first, step), :] = block
        put_rows(block, first)

    def product(left_ref, right_ref, row):
        return dot_nn(left_ref[pl.ds(row, side), :], right_ref[:, pl.ds(row, size - row)])

    def advance(last):
        for row in starts:
            here, there = pl.ds(row, side), pl.ds(row, size - row)
            square = product(gram_l, gram_r, row)
            poly = newton_two * gram[here, there] + newton_three * square
            store(None if last else poly_l, poly_r, poly, row)
        if not last:
            for row in starts:
                here, there = pl.ds(row, side), pl.ds(row, size - row)
                block = newton_one * gram[here, there] + product(poly_l, gram_r, row)
                half[here, there] = block
                store(half_l, None, block, row)
        for first, step in row_steps:
            here = pl.ds(first, step)
            block = newton_one * rows[here, :] + dot_nn(rows_l[here, :], poly_r[...])
            if last:
                out[here, :] = block.astype(out.dtype)
            else:
                rows[here, :] = block
                put_rows(block, first)
        if not last:
            for row in starts:
                here, there = pl.ds(row, side), pl.ds(row, size - row)
                block = newton_one * half[here, there] + product(half_l, poly_r, row)
                gram[here, there] = block
                store(gram_l, gram_r, block, row)

    def turn(_, carry):
        advance(False)
        return carry

    lax.fori_loop(0, 4, turn, 0)
    advance(True)


def newton_chain(gram, rows, dtype):
    size, count = rows.shape[1], rows.shape[0]
    wide, tall = ((size, 3 * size), bf16), ((3 * size, size), bf16)
    shapes = [((size, size), f32), ((count, size), f32), ((size, size), f32)]
    shapes = shapes + [wide, tall, wide, tall, wide, ((count, 3 * size), bf16)]
    whole = pl.BlockSpec(memory_space=pltpu.VMEM)
    return pl.pallas_call(
        chain_kernel,
        out_shape=jax.ShapeDtypeStruct(rows.shape, dtype),
        in_specs=[whole] * 2,
        out_specs=whole,
        scratch_shapes=[pltpu.VMEM(*shape) for shape in shapes],
        compiler_params=pltpu.CompilerParams(vmem_limit_bytes=56 * 1024 * 1024),
        cost_estimate=pl.CostEstimate(
            flops=5 * (13 * size + 5 * count) * size * size,
            bytes_accessed=8 * gram.size,
            transcendentals=0,
        ),
    )(gram, rows)


def body(
    query_ids,
    passage_ids,
    passage_len,
    positives,
    domains,
    table,
    table_m,
    table_v,
    pos_table,
    pos_m,
    pos_v,
    vector,
    vector_m,
    vector_v,
    w_qkv,
    m_qkv,
    w_attn,
    m_attn,
    w_in,
    m_in,
    w_out,
    m_out,
    w_proj,
    m_proj,
):
    blocks = lax.axis_size("blk")
    narrow = lax.axis_size("narrow")
    devices = blocks * narrow
    both = ("blk", "narrow")
    myself = lax.axis_index("blk")
    shard_rows = table.shape[0]
    micro_count, _, query_len = query_ids.shape
    span = passage_ids.shape[2]
    length = query_len + span
    tokens = micro_count * length

    side = D // narrow
    vector_cols = vector.shape[1] // side
    small = jnp.concatenate(
        [
            low(pos_table).T,
            low(w_proj).T,
            low(vector).reshape(side, vector_cols),
            jnp.zeros((side, D - span - VDIM - vector_cols), bf16),
        ],
        axis=1,
    )


    def gather(shard):
        return lax.all_gather(shard, "narrow", axis=0, tiled=True)


    def gather(shard):
        return lax.all_gather(shard, "narrow", axis=0, tiled=True)

    first = gather(jnp.concatenate([small, low(w_attn).T], axis=1))
    small, attn_t = first[:, :D], first[:, D:]
    qkv_t = gather(low(w_qkv).T)
    in_t = gather(low(w_in).T)
    out_t = gather(low(w_out).T)
    pos = small[:, :span].T.astype(f32)
    proj_t = small[:, span : span + VDIM]
    gains = small[:, span + VDIM : span + VDIM + vector_cols].reshape(-1).astype(f32)
    bounds = [0, D, 2 * D, 3 * D, 4 * D, 5 * D, 6 * D, 7 * D, 7 * D + FF, 8 * D + FF, 9 * D + FF]
    bounds = bounds + [10 * D + FF]
    pieces = [gains[None, bounds[index] : bounds[index + 1]] for index in range(11)]
    qkv_bias = jnp.concatenate([pieces[2], jnp.zeros_like(pieces[2]), pieces[3]], axis=1)

    slots = round_up(SLOT_CAPS.get(shard_rows, tokens), 8)
    ids = jnp.concatenate([query_ids[:, 0], passage_ids[:, 0]], axis=1).reshape(tokens)
    owner = ids // shard_rows
    local_id = ids - owner * shard_rows
    is_owner = owner[:, None] == jnp.arange(devices, dtype=jnp.int32)[None]
    before = jnp.arange(tokens)[:, None] > jnp.arange(tokens)[None]
    earlier = dot_nn(before.astype(bf16), is_owner.astype(bf16))
    rank = jnp.sum(jnp.where(is_owner, earlier, 0.0), axis=1).astype(jnp.int32)
    place = owner * slots + rank
    picks = (place[:, None] == jnp.arange(devices * slots, dtype=jnp.int32)[None]).astype(bf16)
    picks_t = (jnp.arange(devices * slots, dtype=jnp.int32)[:, None] == place[None]).astype(bf16)
    picks = lax.optimization_barrier(picks)
    digits = jnp.stack([local_id // 32, local_id % 32], axis=1).astype(bf16)
    asked = dot_tn(digits, picks)
    asked = (asked[0] * 32.0 + asked[1]).astype(jnp.int32).reshape(devices, slots)
    wanted = lax.all_to_all(asked, both, 0, 0, tiled=True).reshape(devices * slots)
    chosen = (wanted[:, None] == jnp.arange(shard_rows, dtype=jnp.int32)[None]).astype(bf16)
    chosen_t = (jnp.arange(shard_rows, dtype=jnp.int32)[:, None] == wanted[None]).astype(bf16)
    chosen = lax.optimization_barrier(chosen)
    sent_rows = low(dot_nn(chosen, low(table))).reshape(devices, slots, D)
    got_rows = lax.all_to_all(sent_rows, both, 0, 0, tiled=True).reshape(devices * slots, D)
    token_rows = dot_nn(picks, got_rows)

    per = blocks // MATRICES
    turn_of = myself // per
    wide_rows = FF // devices

    def padded(rows):
        spare = wide_rows - rows.shape[-2]
        return jnp.pad(rows, ((0, 0),) * (rows.ndim - 2) + ((0, spare), (0, 0)))

    old = [padded(member.T.reshape(blocks, -1, D)) for member in (m_qkv, m_attn, m_in, m_out)]
    old = lax.dynamic_index_in_dim(jnp.stack(old), turn_of, 0, keepdims=False).reshape(-1, D)
    token_rows, old, picks_t, chosen_t = tie(token_rows, old, picks_t, chosen_t)

    lens = passage_len[:, 0]
    pos_rows = jnp.concatenate([pos[:query_len], pos] * micro_count, axis=0)
    x, x_hat, x_scale = norm_forward(token_rows + pos_rows, pieces[0], pieces[1])
    x_low = low(x)
    qkv = low(dot_nt(x_low, qkv_t) + qkv_bias)
    context, norms = attention_forward(lens, qkv, query_len, span)
    heads = round_up(HEADS, 8)
    norms = norms.reshape(micro_count, length, 128)[:, :, :heads].transpose(0, 2, 1)
    norms = jnp.concatenate([norms[:, :, query_len:], norms[:, :, :query_len]], axis=2)
    h, h_hat, h_scale = norm_forward(
        x + dot_nt(context, attn_t) + pieces[4], pieces[5], pieces[6]
    )
    h_low = low(h)
    wide = lax.optimization_barrier(dot_nt(h_low, in_t) + pieces[7])
    gelu_value, gelu_slope = gelu_parts(wide)
    f_low, gelu_slope = tie(low(gelu_value), low(gelu_slope))
    o, o_hat, o_scale = norm_forward(h + dot_nn(f_low, out_t) + pieces[8], pieces[9], pieces[10])
    o_low = low(o)
    e = dot_nn(o_low, proj_t)
    e_scale = lax.rsqrt(jnp.sum(e * e, axis=-1, keepdims=True) + 1e-06)
    vecs = low(e * e_scale)

    labels = domains[:, 0]
    targets = positives[:, 0]
    spots = jnp.arange(blocks, dtype=jnp.int32)
    chosen_label = jnp.sum(
        jnp.where(targets[:, :, None] == spots[None, None], labels[:, None, :], 0), axis=-1
    )

    def spread(mask):
        mask = mask.astype(f32).transpose(1, 0, 2).reshape(blocks, micro_count * blocks, 1)
        return jnp.broadcast_to(mask, (blocks, micro_count * blocks, 128))

    allowed = spread(labels[:, :, None] == chosen_label[:, None, :])
    hits = spread(targets[:, None, :] == spots[None, :, None])
    vecs, allowed, hits = tie(vecs, allowed, hits)
    by_micro = vecs.reshape(micro_count, length, VDIM)
    cycle = by_micro[:, :query_len].reshape(micro_count * query_len, VDIM)
    cycle = share_all(cycle, "blk", blocks).reshape(blocks, micro_count * query_len, VDIM)
    share, scores = score_forward(lens, cycle, vecs, query_len, span)
    every = share_all(scores.reshape(micro_count * blocks, 128), "blk", blocks)
    every = every.reshape(blocks, micro_count * blocks, 128)
    loss_part, d_passage, d_cycle = score_backward(
        myself, every, allowed, hits, share, cycle, vecs, query_len, span
    )
    loss_part = loss_part[0, 0]
    d_query = jnp.sum(lax.all_to_all(d_cycle, "blk", 0, 0, tiled=True), axis=0)
    d_query = d_query.reshape(micro_count, query_len, VDIM)
    d_vecs = jnp.concatenate([d_query, d_passage], axis=1).reshape(tokens, VDIM)

    def reduction(pieces, wire):
        return Reduction(pieces[1::2], pieces[0::2], narrow, blocks, wire)

    def column_sum(values):
        return jnp.sum(values, axis=0)

    d_vecs = low(d_vecs).astype(f32)
    inner = jnp.sum(e * d_vecs, axis=-1, keepdims=True)
    d_e = low(e_scale * d_vecs - e * (e_scale * e_scale * e_scale * inner))
    g_proj = dot_tn(o_low, d_e)
    d_o = low(dot_nt(d_e, proj_t)).astype(f32)
    g_gain_o, g_shift_o = column_sum(d_o * o_hat), column_sum(d_o)
    d_sum_o = norm_backward(d_o, o_hat, o_scale, pieces[9])
    g_bias_out = column_sum(d_sum_o)
    d_y = low(d_sum_o)
    place = lax.axis_index("narrow")
    low_bit = place & 1
    g_out = dot_tn(f_low, d_y).reshape(narrow // 2, 2, -1, D)
    out_sent = lax.dynamic_index_in_dim(g_out, 1 - low_bit, 1, keepdims=False)
    d_y, out_sent, g_out = tie(d_y, out_sent, g_out)
    out_got = swap(out_sent, "narrow", narrow, 1)
    d_f = low(dot_nt(d_y, out_t)).astype(f32)
    d_wide = d_f * gelu_slope.astype(f32)
    g_bias_in = column_sum(d_wide)
    d_wide = low(d_wide)
    d_wide, out_got = tie(d_wide, out_got)
    g_out = lax.dynamic_index_in_dim(g_out, low_bit, 1, keepdims=False) + out_got
    g_out = low(g_out.reshape(-1, D))
    d_wide, g_out = tie(d_wide, g_out)
    if narrow > 2:
        groups = [list(range(bit, narrow, 2)) for bit in range(2)]
        g_out = lax.psum_scatter(
            g_out, "narrow", scatter_dimension=0, axis_index_groups=groups, tiled=True
        )
    sum_in = reduction(relative(dot_tn(d_wide, h_low), narrow), bf16)
    d_wide, sum_in.sent = tie(d_wide, sum_in.sent)
    sum_in.across_core()
    d_wide, sum_in.kept = tie(d_wide, sum_in.kept)
    sum_in.prepare()
    d_wide, sum_in.outgoing, sum_in.kept = tie(d_wide, sum_in.outgoing, sum_in.kept)
    sum_in.send()
    d_h = d_sum_o + low(dot_nn(d_wide, in_t)).astype(f32)
    g_gain_h, g_shift_h = column_sum(d_h * h_hat), column_sum(d_h)
    d_sum_h = norm_backward(d_h, h_hat, h_scale, pieces[5])
    g_bias_attn = column_sum(d_sum_h)
    d_a = low(d_sum_h)
    sum_attn = reduction(relative(dot_tn(d_a, context), narrow), bf16)
    d_a, sum_attn.sent, g_out = tie(d_a, sum_attn.sent, g_out)
    g_out = lax.psum_scatter(g_out.astype(f32), "blk", scatter_dimension=0, tiled=True)
    sum_attn.across_core()
    d_context = low(dot_nn(d_a, attn_t))
    d_context, sum_attn.got = tie(d_context, sum_attn.got)
    sum_attn.across_narrow()
    head_of = jnp.arange(D)[None] // HDIM == jnp.arange(heads)[:, None]
    inner = lax.dot_general(
        head_of.astype(f32),
        d_context.astype(f32) * context.astype(f32),
        (((1,), (1,)), ((), ())),
        precision=lax.Precision.HIGH,
        preferred_element_type=f32,
    )
    inner = inner.reshape(heads, micro_count, length).transpose(1, 0, 2)
    inner = jnp.concatenate([inner[:, :, query_len:], inner[:, :, :query_len]], axis=2)
    d_qkv = attention_backward(lens, qkv, d_context, norms, inner, query_len, span)
    d_qkv, sum_in.got, sum_attn.got = tie(d_qkv, sum_in.got, sum_attn.got)
    g_in = sum_in.total()
    d_qkv, g_in = tie(d_qkv, g_in)
    g_in = lax.psum_scatter(g_in, "blk", scatter_dimension=0, tiled=True)
    d_x = d_sum_h + low(dot_nn(d_qkv, qkv_t)).astype(f32)
    d_rows = norm_backward(d_x, x_hat, x_scale, pieces[0])

    back_rows = low(dot_nn(picks_t, low(d_rows))).reshape(devices, slots, D)
    back_rows, d_rows, d_x, d_qkv, g_proj = tie(back_rows, d_rows, d_x, d_qkv, g_proj)
    back_rows = lax.all_to_all(back_rows, both, 0, 0, tiled=True).reshape(devices * slots, D)
    sum_qkv = reduction(relative(dot_tn(d_qkv, x_low), narrow), bf16)
    d_qkv, d_rows, d_x, sum_qkv.sent = tie(d_qkv, d_rows, d_x, sum_qkv.sent)
    sum_qkv.across_core()
    sum_qkv.across_narrow()
    early = (g_bias_attn, g_gain_h, g_shift_h, g_bias_in, g_bias_out, g_gain_o, g_shift_o)
    tail = late_sums(d_rows, d_x, x_hat, d_qkv, g_proj, early, query_len, span, micro_count)
    sum_tail = reduction(relative(tail, narrow), f32)
    sum_tail.across_core()
    sum_tail.across_narrow()
    tail = sum_tail.total()
    spare_high = lax.optimization_barrier(low(tail[:, span:]))
    tail = [low(tail[:, :span]), spare_high, low(tail[:, span:] - spare_high.astype(f32))]
    tail = jnp.concatenate(tail, axis=1).reshape(blocks, -1)
    tail_size = tail.shape[1]
    tail = jnp.pad(tail, ((0, 0), (0, round_up(tail_size, 16 * D) - tail_size)))
    merged = [low(member.total()).reshape(blocks, -1, D) for member in (sum_qkv, sum_attn)]
    merged = jnp.concatenate(merged + [tail.reshape(blocks, -1, D)], axis=1)
    merged, back_rows = tie(merged, back_rows)
    merged = lax.all_to_all(merged, "blk", 0, 0, tiled=True)
    table_grad = dot_nn(chosen_t, back_rows)
    table_square = jnp.sum(table_grad * table_grad)
    merged = jnp.sum(merged.astype(f32), axis=0)
    attn_rows = D // devices
    qkv_rows = 3 * attn_rows
    g_qkv, g_attn = merged[:qkv_rows], merged[qkv_rows : qkv_rows + attn_rows]
    g_tail = merged[qkv_rows + attn_rows :].reshape(-1)[:tail_size].reshape(attn_rows, -1)
    spare = g_tail[:, span : span + 128 + VDIM] + g_tail[:, span + 128 + VDIM :]
    g_tail = jnp.concatenate([g_tail[:, :span], spare], axis=1)
    g_qkv, g_attn, g_out, g_in, g_tail, table_square = tie(
        g_qkv, g_attn, g_out, g_in, g_tail, table_square
    )

    sends = [padded(low(member)) for member in (g_qkv, g_attn, g_in, g_out)]
    sends = jnp.repeat(jnp.stack(sends), per, axis=0)
    taken = lax.all_to_all(sends, "blk", 0, 0, tiled=True)

    def square_sum(values):
        values = values.astype(f32)
        return jnp.sum(values * values)

    local_square = (
        table_square
        + square_sum(g_out)
        + square_sum(g_in)
        + square_sum(g_qkv)
        + square_sum(g_attn)
        + square_sum(g_tail)
    )
    lane = lax.broadcasted_iota(jnp.int32, (8, 128), 1)
    pair = jnp.where(lane == 0, local_square, jnp.where(lane == 1, loss_part, 0.0))
    sums = sum_everywhere(pair, (("narrow", narrow), ("blk", blocks)))
    loss = sums[0, 1]
    grad_norm = jnp.sqrt(sums[0, 0])
    factor = jnp.minimum(1.0, clip_limit / (grad_norm + 1e-06))

    packed = [low(member) for member in (g_qkv, g_attn, g_in, g_out, g_tail)]
    complete = lax.all_gather(jnp.concatenate(packed, axis=0), "blk", axis=0, tiled=False)
    moment, gram = packed_gram(factor, old, taken.reshape(-1, D))
    gram = sum_group(gram, narrow, 1, blocks)
    half = moment.shape[0] // per
    moment = lax.dynamic_slice_in_dim(moment, myself % per * half, half, axis=0)
    ortho = newton_chain(gram, moment, bf16)
    ortho, complete = tie(ortho, complete)
    ortho = lax.all_gather(ortho, "blk", axis=0, tiled=False)
    ortho = ortho.reshape(MATRICES, blocks, wide_rows, D)
    matrix_rows = (qkv_rows, attn_rows, wide_rows, wide_rows)

    def turned(rows):
        return rows.reshape(-1, D).T.astype(f32)

    grads, first = [], 0
    for rows in matrix_rows:
        grads.append(turned(complete[:, first : first + rows]))
        first += rows
    tail_all = complete[:, first:].reshape(side, -1)
    grad_pos = tail_all[:, :span].T.astype(f32)
    grad_proj = tail_all[:, span + 128 :].T.astype(f32)
    grad_vector = tail_all[:, span : span + 128].T
    grad_bias = grad_vector[4:5].astype(f32)
    place = lax.axis_index("narrow")
    whole_vector = jnp.zeros((narrow,) + grad_vector.shape, bf16)
    for offset, piece in enumerate(gather_relative(grad_vector, narrow)):
        whole_vector = lax.dynamic_update_index_in_dim(whole_vector, piece, place ^ offset, 0)
    whole_vector = whole_vector.transpose(1, 0, 2)[:vector_cols].reshape(1, -1).astype(f32)
    grad_vector = lax.dynamic_slice_in_dim(
        whole_vector, place * vector.shape[1], vector.shape[1], axis=1
    )
    proj_rows, gram_proj = packed_gram(factor, m_proj.T, grad_proj.T)
    ortho_proj = newton_chain(sum_group(gram_proj, narrow, 1, blocks), proj_rows, f32)
    table_new, table_m_new, table_v_new = adam_step(
        table, table_m, table_v, factor * table_grad, adam_rate
    )
    pos_new, pos_m_new, pos_v_new = adam_step(
        pos_table, pos_m, pos_v, factor * grad_pos, adam_rate
    )
    vector_new, vector_m_new, vector_v_new = adam_step(
        vector, vector_m, vector_v, factor * grad_vector, vector_rate
    )
    olds = (m_qkv, m_attn, m_in, m_out, m_proj)
    grads = grads + [grad_proj]
    moments = [muon_moment * before + factor * grad for before, grad in zip(olds, grads)]
    masters = (w_qkv, w_attn, w_proj)
    orthos = (turned(ortho[0, :, :qkv_rows]), turned(ortho[1, :, :attn_rows]), ortho_proj.T)
    updated = []
    for weight, ortho_part, rate in zip(masters, orthos, (muon_rate, attn_rate, muon_rate)):
        long_side = max(weight.shape[0], weight.shape[1] * narrow)
        updated.append(weight - rate * (0.2 * long_side**0.5 * ortho_part + weight_decay * weight))
    wide_orthos = [ortho[index].reshape(-1, D) for index in (2, 3)]
    in_new, out_new = update_wide((w_in, w_out), wide_orthos, muon_rate, 0.2 * FF**0.5)
    updated = [updated[0], updated[1], in_new, out_new, updated[2]]
    return (
        loss,
        grad_norm,
        table_new,
        table_m_new,
        table_v_new,
        pos_new,
        pos_m_new,
        pos_v_new,
        vector_new,
        vector_m_new,
        vector_v_new,
        updated[0],
        moments[0],
        updated[1],
        moments[1],
        updated[2],
        moments[2],
        updated[3],
        moments[3],
        updated[4],
        moments[4],
        factor * grad_bias,
    )


def solution(mesh):
    ids = P(None, ("blk", "narrow"), None)
    rows = P(("blk", "narrow"), None)
    cols = P(None, "narrow")
    group = P(None, "narrow", None)
    in_specs = (ids, ids, P(None, ("blk", "narrow")), group, group) + (rows,) * 3 + (cols,) * 16
    out_specs = (P(), P()) + (rows,) * 3 + (cols,) * 17
    return jax.shard_map(body, mesh=mesh, in_specs=in_specs, out_specs=out_specs, check_vma=False)
```

```python
import functools

import jax
import jax.numpy as jnp
from jax import lax
from jax.experimental import pallas as pl
from jax.experimental.pallas import tpu as pltpu
from jax.sharding import PartitionSpec as P

D = 768
HEADS = 12
HDIM = 64
FF = 3072
VDIM = 128
STEP = 10
MATRICES = 4

norm_eps = 1e-12
smoothing = 0.1
masked = -1e30
newton_one = 3.4445
newton_two = -4.775
newton_three = 2.0315
muon_rate = 0.1
attn_rate = 1.0
muon_moment = 0.95
weight_decay = 0.01
adam_rate = 0.02
vector_rate = 0.25
beta_one = 0.9
beta_two = 0.95
adam_eps = 1e-08
clip_limit = 0.05

bf16 = jnp.bfloat16
f32 = jnp.float32
SLOT_CAPS = {960: 36, 120: 7}


def round_up(value, step):
    return -(-value // step) * step


def dot_nn(left, right):
    return lax.dot_general(left, right, (((1,), (0,)), ((), ())), preferred_element_type=f32)


def dot_nt(left, right):
    return lax.dot_general(left, right, (((1,), (1,)), ((), ())), preferred_element_type=f32)


def dot_tn(left, right):
    return lax.dot_general(left, right, (((0,), (0,)), ((), ())), preferred_element_type=f32)


def low(values):
    return values.astype(bf16)


def norm_forward(values, gain, shift):
    centred = values - jnp.mean(values, axis=-1, keepdims=True)
    spread = jnp.mean(centred * centred, axis=-1, keepdims=True)
    scale = lax.rsqrt(spread + norm_eps)
    hat = centred * scale
    return hat * gain + shift, hat, scale


def norm_backward(grad, hat, scale, gain):
    d_hat = grad * gain
    first = jnp.mean(d_hat, axis=-1, keepdims=True)
    second = jnp.mean(d_hat * hat, axis=-1, keepdims=True)
    return scale * (d_hat - first - hat * second)


def gelu_parts(values):
    cdf = 0.5 * (1.0 + lax.erf(values * (0.5**0.5)))
    density = jnp.exp(-0.5 * values * values) * 0.3989422804014327
    return values * cdf, cdf + values * density


def attention_forward_kernel(
    lens_ref, qkv_ref, out_ref, norm_ref, scores_one, scores_two, share_one, share_two, *, query_len, span
):
    used = lens_ref[pl.program_id(0)]
    bias_long = jnp.where(lax.broadcasted_iota(jnp.int32, (1, span), 1) < used, 0.0, masked)
    bias_short = jnp.zeros((1, query_len), f32)
    lane_of = lax.broadcasted_iota(jnp.int32, (16, 128), 1)
    norm_ref[...] = jnp.zeros_like(norm_ref)

    def attend(first, count, lane, half, bias, head, scores_ref, share_ref):
        rows, span_of = pl.ds(first, count), pl.ds(0, count)
        queries = qkv_ref[rows, pl.ds(lane, 128)][:, half] * bf16(HDIM**-0.5)
        keys = qkv_ref[rows, pl.ds(lane + D, 128)][:, half]
        values = qkv_ref[rows, pl.ds(lane + 2 * D, 128)][:, half]
        scores_ref[span_of, span_of] = dot_nt(queries, keys)
        for step in range(0, count, 16):
            here = pl.ds(step, 16)
            scores = scores_ref[here, span_of] + bias
            peak = jnp.max(scores, axis=-1, keepdims=True)
            exponent = jnp.exp(scores - peak)
            total = jnp.sum(exponent, axis=-1, keepdims=True)
            share_ref[here, span_of] = low(exponent * (1.0 / total))
            there = pl.ds(first + step, 16)
            norm_ref[there, :] = jnp.where(lane_of == head, peak + jnp.log(total), norm_ref[there, :])
        return dot_nn(share_ref[span_of, span_of], values)

    def pair(index, carry):
        lane = pl.multiple_of(index * 128, 128)
        for first, count, bias in ((0, query_len, bias_short), (query_len, span, bias_long)):
            one = attend(
                first, count, lane, slice(0, HDIM), bias, 2 * index, scores_one, share_one
            )
            two = attend(
                first, count, lane, slice(HDIM, 128), bias, 2 * index + 1, scores_two, share_two
            )
            out_ref[pl.ds(first, count), pl.ds(lane, 128)] = low(jnp.concatenate([one, two], axis=1))
        return carry

    lax.fori_loop(0, HEADS // 2, pair, 0)


def attention_forward(lens, qkv, query_len, span):
    length = query_len + span
    tokens = qkv.shape[0]
    micro_count = tokens // length
    block = pl.BlockSpec((length, 3 * D), lambda micro, lens: (micro, 0))
    square = [pltpu.VMEM((span, span), f32)] * 2 + [pltpu.VMEM((span, span), bf16)] * 2
    return pl.pallas_call(
        functools.partial(attention_forward_kernel, query_len=query_len, span=span),
        out_shape=(
            jax.ShapeDtypeStruct((tokens, D), bf16),
            jax.ShapeDtypeStruct((tokens, 128), f32),
        ),
        grid_spec=pltpu.PrefetchScalarGridSpec(
            num_scalar_prefetch=1,
            grid=(micro_count,),
            in_specs=[block],
            out_specs=(
                pl.BlockSpec((length, D), lambda micro, lens: (micro, 0)),
                pl.BlockSpec((length, 128), lambda micro, lens: (micro, 0)),
            ),
            scratch_shapes=square,
        ),
        compiler_params=pltpu.CompilerParams(vmem_limit_bytes=48 * 1024 * 1024),
        cost_estimate=pl.CostEstimate(
            flops=8 * micro_count * HEADS * span * span * HDIM,
            bytes_accessed=tokens * 8 * D,
            transcendentals=micro_count * HEADS * span * span,
        ),
    )(lens, qkv)


def attention_backward_kernel(
    lens_ref,
    qkv_ref,
    grad_ref,
    norm_ref,
    inner_ref,
    out_ref,
    scores_one,
    scores_two,
    slopes_one,
    slopes_two,
    share_one,
    share_two,
    d_one,
    d_two,
    *,
    query_len,
    span,
):
    used = lens_ref[pl.program_id(0)]
    bias_long = jnp.where(lax.broadcasted_iota(jnp.int32, (span, 1), 0) < used, 0.0, masked)
    bias_short = jnp.zeros((query_len, 1), f32)

    def attend(first, count, lane, half, bias, head, scores_ref, slopes_ref, share_ref, d_ref):
        rows, span_of = pl.ds(first, count), pl.ds(0, count)
        queries = qkv_ref[rows, pl.ds(lane, 128)][:, half] * bf16(HDIM**-0.5)
        keys = qkv_ref[rows, pl.ds(lane + D, 128)][:, half]
        values = qkv_ref[rows, pl.ds(lane + 2 * D, 128)][:, half]
        grads = grad_ref[rows, pl.ds(lane, 128)][:, half]
        lanes = slice(0, count) if first else slice(span, span + count)
        norm = norm_ref[0, pl.ds(head, 1), :][:, lanes]
        inner = inner_ref[0, pl.ds(head, 1), :][:, lanes]
        scores_ref[span_of, span_of] = dot_nt(keys, queries)
        slopes_ref[span_of, span_of] = dot_nt(values, grads)
        for step in range(0, count, 16):
            here = pl.ds(step, 16)
            scores = scores_ref[here, span_of] + bias[step : step + 16]
            share = jnp.exp(scores - norm)
            share_ref[here, span_of] = low(share)
            d_ref[here, span_of] = low(share * (slopes_ref[here, span_of] - inner))
        d_scores = d_ref[span_of, span_of]
        d_values = dot_nn(share_ref[span_of, span_of], grads)
        d_keys = dot_nn(d_scores, queries)
        d_queries = dot_tn(d_scores, keys) * HDIM**-0.5
        return d_queries, d_keys, d_values

    def pair(index, carry):
        lane = pl.multiple_of(index * 128, 128)
        for first, count, bias in ((0, query_len, bias_short), (query_len, span, bias_long)):
            one = attend(
                first,
                count,
                lane,
                slice(0, HDIM),
                bias,
                2 * index,
                scores_one,
                slopes_one,
                share_one,
                d_one,
            )
            two = attend(
                first,
                count,
                lane,
                slice(HDIM, 128),
                bias,
                2 * index + 1,
                scores_two,
                slopes_two,
                share_two,
                d_two,
            )
            for part in range(3):
                both = jnp.concatenate([one[part], two[part]], axis=1)
                out_ref[pl.ds(first, count), pl.ds(lane + part * D, 128)] = low(both)
        return carry

    lax.fori_loop(0, HEADS // 2, pair, 0)


def attention_backward(lens, qkv, grad, norm, inner, query_len, span):
    length = query_len + span
    tokens = qkv.shape[0]
    micro_count = tokens // length
    heads = norm.shape[1]

    def block(width):
        return pl.BlockSpec((length, width), lambda micro, lens: (micro, 0))

    row = pl.BlockSpec((1, heads, length), lambda micro, lens: (micro, 0, 0))
    square = [pltpu.VMEM((span, span), f32)] * 4 + [pltpu.VMEM((span, span), bf16)] * 4
    return pl.pallas_call(
        functools.partial(attention_backward_kernel, query_len=query_len, span=span),
        out_shape=jax.ShapeDtypeStruct((tokens, 3 * D), bf16),
        grid_spec=pltpu.PrefetchScalarGridSpec(
            num_scalar_prefetch=1,
            grid=(micro_count,),
            in_specs=[block(3 * D), block(D), row, row],
            out_specs=block(3 * D),
            scratch_shapes=square,
        ),
        compiler_params=pltpu.CompilerParams(vmem_limit_bytes=48 * 1024 * 1024),
        cost_estimate=pl.CostEstimate(
            flops=20 * micro_count * HEADS * span * span * HDIM,
            bytes_accessed=tokens * 14 * D,
            transcendentals=micro_count * HEADS * span * span,
        ),
    )(lens, qkv, grad, norm, inner)


def update_kernel(*refs, rate, scale):
    count = len(refs) // 3
    for weight, ortho, out in zip(refs[:count], refs[count : 2 * count], refs[2 * count :]):
        turned = ortho[...].astype(f32).T
        out[...] = weight[...] - rate * (scale * turned + weight_decay * weight[...])


def update_wide(weights, orthos, rate, scale):
    rows, columns = weights[0].shape
    step = 128
    weight_spec = pl.BlockSpec((rows, step), lambda place: (0, place))
    ortho_spec = pl.BlockSpec((step, rows), lambda place: (place, 0))
    count = len(weights)
    return pl.pallas_call(
        functools.partial(update_kernel, rate=rate, scale=scale),
        grid=(columns // step,),
        in_specs=[weight_spec] * count + [ortho_spec] * count,
        out_specs=(weight_spec,) * count,
        out_shape=(jax.ShapeDtypeStruct((rows, columns), f32),) * count,
        compiler_params=pltpu.CompilerParams(vmem_limit_bytes=32 * 1024 * 1024),
        cost_estimate=pl.CostEstimate(
            flops=4 * count * rows * columns,
            bytes_accessed=10 * count * rows * columns,
            transcendentals=0,
        ),
    )(*weights, *orthos)


def score_kernel(lens_ref, cycle_ref, vecs_ref, share_ref, scores_ref, *, query_len, span):
    micro = pl.program_id(0)
    blocks = cycle_ref.shape[0]
    mine = pl.ds(pl.multiple_of(micro * query_len, query_len), query_len)
    queries = jnp.concatenate([cycle_ref[place, mine, :] for place in range(blocks)], axis=0)
    first = pl.multiple_of(micro * (query_len + span) + query_len, query_len)
    sims = dot_nt(queries, vecs_ref[pl.ds(first, span), :])
    used = lax.broadcasted_iota(jnp.int32, (1, span), 1) < lens_ref[micro]
    scaled = jnp.where(used, sims / smoothing, masked)
    summit = jnp.max(scaled, axis=-1, keepdims=True)
    exponent = jnp.exp(scaled - summit)
    total = jnp.sum(exponent, axis=-1, keepdims=True)
    share_ref[0] = exponent / total
    smooth = smoothing * (summit + jnp.log(total))
    smooth = jnp.broadcast_to(smooth, (blocks * query_len, 128))
    scores_ref[0] = jnp.sum(smooth.reshape(blocks, query_len, 128), axis=1)


def score_forward(lens, cycle, vecs, query_len, span):
    blocks, micro_count = cycle.shape[0], lens.shape[0]
    rows = blocks * query_len
    return pl.pallas_call(
        functools.partial(score_kernel, query_len=query_len, span=span),
        out_shape=(
            jax.ShapeDtypeStruct((micro_count, rows, span), f32),
            jax.ShapeDtypeStruct((micro_count, blocks, 128), f32),
        ),
        grid_spec=pltpu.PrefetchScalarGridSpec(
            num_scalar_prefetch=1,
            grid=(micro_count,),
            in_specs=[
                pl.BlockSpec(cycle.shape, lambda micro, lens: (0, 0, 0)),
                pl.BlockSpec(vecs.shape, lambda micro, lens: (0, 0)),
            ],
            out_specs=(
                pl.BlockSpec((1, rows, span), lambda micro, lens: (micro, 0, 0)),
                pl.BlockSpec((1, blocks, 128), lambda micro, lens: (micro, 0, 0)),
            ),
        ),
        compiler_params=pltpu.CompilerParams(vmem_limit_bytes=48 * 1024 * 1024),
        cost_estimate=pl.CostEstimate(
            flops=2 * micro_count * rows * span * VDIM,
            bytes_accessed=4 * micro_count * rows * span,
            transcendentals=micro_count * rows * span,
        ),
    )(lens, cycle, vecs)


def loss_kernel(
    me_ref,
    every_ref,
    allowed_ref,
    hits_ref,
    share_ref,
    cycle_ref,
    vecs_ref,
    loss_ref,
    passage_ref,
    query_ref,
    *,
    query_len,
    span,
):
    me = me_ref[0]
    blocks = cycle_ref.shape[0]
    micro_count = share_ref.shape[0]
    every = every_ref[...]
    allowed = allowed_ref[...] > 0.0
    peak = jnp.max(jnp.where(allowed, every, masked), axis=0)
    mass = jnp.sum(jnp.where(allowed, jnp.exp(every - peak[None]), 0.0), axis=0)
    log_total = peak + jnp.log(mass)
    matched = jnp.sum(jnp.where(hits_ref[...] > 0.0, every, 0.0), axis=0)
    row = lax.broadcasted_iota(jnp.int32, log_total.shape, 0)
    mine = jnp.where(row % blocks == me, log_total - matched, 0.0)
    loss_ref[...] = jnp.broadcast_to(jnp.sum(mine, axis=0, keepdims=True), loss_ref.shape)
    d_scores = jnp.where(allowed_ref[me] > 0.0, jnp.exp(every_ref[me] - log_total), 0.0)
    d_scores = d_scores - hits_ref[me]
    for micro in range(micro_count):
        own = d_scores[micro * blocks : (micro + 1) * blocks]
        own = jnp.broadcast_to(own[:, None, :], (blocks, query_len, 128))
        own = own.reshape(blocks * query_len, 128)[:, 0:1]
        d_sims = low(own * share_ref[micro])
        here = slice(micro * query_len, (micro + 1) * query_len)
        queries = jnp.concatenate([cycle_ref[place, here, :] for place in range(blocks)], axis=0)
        first = micro * (query_len + span) + query_len
        passage_ref[micro] = dot_tn(d_sims, queries)
        d_queries = dot_nn(d_sims, vecs_ref[first : first + span, :])
        for place in range(blocks):
            rows = slice(place * query_len, (place + 1) * query_len)
            query_ref[place, here, :] = d_queries[rows]


def score_backward(me, every, allowed, hits, share, cycle, vecs, query_len, span):
    micro_count = share.shape[0]
    whole = pl.BlockSpec(memory_space=pltpu.VMEM)
    return pl.pallas_call(
        functools.partial(loss_kernel, query_len=query_len, span=span),
        out_shape=(
            jax.ShapeDtypeStruct((8, 128), f32),
            jax.ShapeDtypeStruct((micro_count, span, VDIM), f32),
            jax.ShapeDtypeStruct(cycle.shape, f32),
        ),
        in_specs=[pl.BlockSpec(memory_space=pltpu.SMEM)] + [whole] * 6,
        out_specs=(whole,) * 3,
        compiler_params=pltpu.CompilerParams(vmem_limit_bytes=48 * 1024 * 1024),
        cost_estimate=pl.CostEstimate(
            flops=4 * share.size * VDIM, bytes_accessed=4 * share.size, transcendentals=0
        ),
    )(me.reshape(1).astype(jnp.int32), every, allowed, hits, share, cycle, vecs)


def tail_kernel(rows_ref, x_ref, hat_ref, qkv_ref, proj_ref, *refs, query_len, span, micro_count):
    out_ref = refs[-1]
    length = query_len + span
    for first in range(0, span, 128):
        block = rows_ref[query_len + first : query_len + first + 128, :]
        for micro in range(1, micro_count):
            start = micro * length + query_len + first
            block = block + rows_ref[start : start + 128, :]
        if first == 0:
            head = rows_ref[0:query_len, :]
            for micro in range(1, micro_count):
                head = head + rows_ref[micro * length : micro * length + query_len, :]
            block = jnp.concatenate([block[:query_len] + head, block[query_len:]], axis=0)
        out_ref[:, first : first + 128] = block.T

    def fold(values):
        return jnp.sum(values.reshape(-1, 8, D), axis=0)

    sums = [jnp.zeros((8, D), f32)] * 4
    for first in range(0, micro_count * length, 32):
        here = pl.ds(first, 32)
        d_x = x_ref[here, :]
        terms = (
            d_x * hat_ref[here, :],
            d_x,
            qkv_ref[here, 0:D].astype(f32),
            qkv_ref[here, 2 * D : 3 * D].astype(f32),
        )
        sums = [total + fold(term) for total, term in zip(sums, terms)]
    sums = [jnp.sum(total, axis=0, keepdims=True) for total in sums]
    for ref in refs[:-1]:
        sums = sums + [ref[:, first : first + D] for first in range(0, ref.shape[1], D)]
    sums.append(jnp.zeros((128 - len(sums), D), f32))
    out_ref[:, span : span + 128] = jnp.concatenate(sums, axis=0).T
    out_ref[:, span + 128 :] = proj_ref[...]


def late_sums(d_rows, d_x, x_hat, d_qkv, g_proj, early, query_len, span, micro_count):
    early = [member.reshape(1, -1) for member in early]
    whole = pl.BlockSpec(memory_space=pltpu.VMEM)
    return pl.pallas_call(
        functools.partial(
            tail_kernel, query_len=query_len, span=span, micro_count=micro_count
        ),
        out_shape=jax.ShapeDtypeStruct((D, span + 128 + VDIM), f32),
        in_specs=[whole] * (5 + len(early)),
        out_specs=whole,
        compiler_params=pltpu.CompilerParams(vmem_limit_bytes=48 * 1024 * 1024),
        cost_estimate=pl.CostEstimate(
            flops=8 * d_rows.size, bytes_accessed=20 * d_rows.size, transcendentals=0
        ),
    )(d_rows, d_x, x_hat, d_qkv, g_proj, *early)


def share_all(value, axes, count):
    spread = jnp.broadcast_to(value[None], (count,) + value.shape)
    return lax.all_to_all(spread, axes, 0, 0, tiled=True)


def swap(value, axis, size, bit):
    return lax.ppermute(value, axis, [(place, place ^ bit) for place in range(size)])


def gather_relative(shard, narrow):
    pieces = {0: shard}
    bit = narrow // 2
    while bit:
        for offset in list(pieces):
            pieces[offset ^ bit] = swap(pieces[offset], "narrow", narrow, bit)
        bit = bit // 2
    return [pieces[offset] for offset in range(narrow)]


def relative(whole, narrow):
    place = lax.axis_index("narrow")
    rows = whole.shape[0] // narrow
    return [
        lax.dynamic_slice_in_dim(whole, (place ^ offset) * rows, rows, axis=0)
        for offset in range(narrow)
    ]


def gram_kernel(factor_ref, old_ref, grad_ref, moment_ref, gram_ref):
    moment = muon_moment * old_ref[...] + factor_ref[0] * grad_ref[...].astype(f32)
    moment_ref[...] = moment
    high, rest = split(moment)
    size = moment.shape[1]
    side = size if gram_ref.shape[0] == size else size // 3

    def part(row):
        left = slice(row, row + side)
        right = slice(row, size)
        return (
            dot_tn(high[:, left], high[:, right])
            + dot_tn(high[:, left], rest[:, right])
            + dot_tn(rest[:, left], high[:, right])
        )

    gram_ref[0:side, :] = part(0)
    if side < size:
        gram_ref[side : 2 * side, 0 : 2 * side] = part(side)
        gram_ref[side : 2 * side, 2 * side : size] = part(2 * side)


def packed_gram(factor, old, grad):
    count, size = old.shape
    whole = pl.BlockSpec(memory_space=pltpu.VMEM)
    packed = size if size < 3 * 128 else 2 * size // 3
    return pl.pallas_call(
        gram_kernel,
        out_shape=(
            jax.ShapeDtypeStruct((count, size), f32),
            jax.ShapeDtypeStruct((packed, size), f32),
        ),
        in_specs=[pl.BlockSpec(memory_space=pltpu.SMEM), whole, whole],
        out_specs=(whole, whole),
        compiler_params=pltpu.CompilerParams(vmem_limit_bytes=48 * 1024 * 1024),
        cost_estimate=pl.CostEstimate(
            flops=4 * count * size * size, bytes_accessed=14 * count * size, transcendentals=0
        ),
    )(factor.reshape(1), old, grad)


def tie(*values):
    return lax.optimization_barrier(values)


class Reduction:
    def __init__(self, sent, kept, narrow, blocks, wire):
        self.narrow, self.blocks, self.wire = narrow, blocks, wire
        self.sent, self.kept = list(sent), list(kept)

    def across_core(self):
        self.got = [swap(member, "narrow", self.narrow, 1) for member in self.sent]

    def prepare(self):
        totals = [kept + got for kept, got in zip(self.kept, self.got)]
        half = len(totals) // 2
        while half > 1:
            for offset in range(half):
                got = swap(totals[offset + half].astype(self.wire), "narrow", self.narrow, 2 * half)
                totals[offset] = totals[offset] + got.astype(f32)
            half = half // 2
        self.kept = totals[0]
        self.outgoing = totals[-1].astype(self.wire)

    def across_narrow(self):
        self.prepare()
        self.send()

    def send(self):
        if self.narrow > 2:
            self.got = swap(self.outgoing, "narrow", self.narrow, 2)
        else:
            self.got = jnp.zeros_like(self.outgoing)

    def total(self):
        return self.kept + self.got.astype(f32)


def sum_everywhere(value, sizes):
    for axis, size in sizes:
        bit = 1
        while bit < size:
            value = value + swap(value, axis, size, bit)
            bit = bit * 2
    return value


def sum_group(value, narrow, per, blocks):
    steps = [("narrow", narrow, 1)]
    steps = steps + [("blk", blocks, 1 << bit) for bit in range(per.bit_length() - 1)]
    for axis, size, bit in steps:
        halves = value.reshape(2, value.shape[0] // 2, value.shape[1])
        mine = (lax.axis_index(axis) // bit) & 1
        sent = lax.dynamic_index_in_dim(halves, 1 - mine, 0, keepdims=False)
        got = swap(sent, axis, size, bit)
        value = lax.dynamic_index_in_dim(halves, mine, 0, keepdims=False) + got
    bit = 2
    while bit < narrow:
        value = value + swap(value, "narrow", narrow, bit)
        bit = bit * 2
    for axis, size, bit in reversed(steps):
        other = swap(value, axis, size, bit)
        lower = (lax.axis_index(axis) // bit) & 1 == 0
        value = jnp.concatenate(
            [jnp.where(lower, value, other), jnp.where(lower, other, value)], axis=0
        )
    return value


def adam_step(weight, first, second, gradient, rate):
    first_new = beta_one * first + (1.0 - beta_one) * gradient
    second_new = beta_two * second + (1.0 - beta_two) * gradient * gradient
    update = (
        first_new
        / (1.0 - beta_one**STEP)
        / (jnp.sqrt(second_new / (1.0 - beta_two**STEP)) + adam_eps)
    )
    return (weight - rate * (update + weight_decay * weight), first_new, second_new)


def split(value):
    high = low(value)
    return high, low(value - high.astype(f32))


def chain_kernel(
    gram_in, rows_in, out, gram, rows, half, gram_l, gram_r, poly_l, poly_r, half_l, rows_l
):
    size, count = gram.shape[0], rows.shape[0]
    parts = 3 if gram_in.shape[0] < size else 1
    side = size // parts

    def put(left_ref, right_ref, value, row, column):
        for piece, first, second in ((value, row, column), (value.T, column, row)):
            high, rest = split(piece)
            width = piece.shape[1]
            if left_ref is not None:
                here = pl.ds(first, piece.shape[0])
                left_ref[here, pl.ds(second, width)] = high
                left_ref[here, pl.ds(size + second, width)] = high
                left_ref[here, pl.ds(2 * size + second, width)] = rest
            if right_ref is not None:
                there = pl.ds(second, width)
                right_ref[pl.ds(first, piece.shape[0]), there] = high
                right_ref[pl.ds(size + first, piece.shape[0]), there] = rest
                right_ref[pl.ds(2 * size + first, piece.shape[0]), there] = high
            if row == column:
                break

    def store(left_ref, right_ref, value, row):
        for place in range(row // side, parts):
            column = place * side
            put(left_ref, right_ref, value[:, column - row : column - row + side], row, column)

    def put_rows(value, first):
        high, rest = split(value)
        here = pl.ds(first, value.shape[0])
        rows_l[here, 0:size] = high
        rows_l[here, size : 2 * size] = high
        rows_l[here, 2 * size : 3 * size] = rest

    def packed(row):
        if parts == 1 or row == 0:
            return gram_in[0:side, :]
        if row == side:
            return gram_in[side : 2 * side, 0 : 2 * side]
        return gram_in[side : 2 * side, 2 * side : size]

    starts = [place * side for place in range(parts)]
    row_steps = [(first, min(256, count - first)) for first in range(0, count, 256)]
    diagonal = lax.broadcasted_iota(jnp.int32, (side, side), 0) == lax.broadcasted_iota(
        jnp.int32, (side, side), 1
    )
    trace = jnp.zeros((1, 1), f32)
    for row in starts:
        block = packed(row)[:, 0:side]
        trace = trace + jnp.sum(jnp.where(diagonal, block, 0.0), axis=(0, 1), keepdims=True)
    scale = 1.0 / (jnp.sqrt(trace) + 1e-07)
    for row in starts:
        block = packed(row) * (scale * scale)
        gram[pl.ds(row, side), pl.ds(row, size - row)] = block
        store(gram_l, gram_r, block, row)
    for first, step in row_steps:
        block = rows_in[pl.ds(first, step), :] * scale
        rows[pl.ds(first, step), :] = block
        put_rows(block, first)

    def product(left_ref, right_ref, row):
        return dot_nn(left_ref[pl.ds(row, side), :], right_ref[:, pl.ds(row, size - row)])

    def advance(last):
        for row in starts:
            here, there = pl.ds(row, side), pl.ds(row, size - row)
            square = product(gram_l, gram_r, row)
            poly = newton_two * gram[here, there] + newton_three * square
            store(None if last else poly_l, poly_r, poly, row)
        if not last:
            for row in starts:
                here, there = pl.ds(row, side), pl.ds(row, size - row)
                block = newton_one * gram[here, there] + product(poly_l, gram_r, row)
                half[here, there] = block
                store(half_l, None, block, row)
        for first, step in row_steps:
            here = pl.ds(first, step)
            block = newton_one * rows[here, :] + dot_nn(rows_l[here, :], poly_r[...])
            if last:
                out[here, :] = block.astype(out.dtype)
            else:
                rows[here, :] = block
                put_rows(block, first)
        if not last:
            for row in starts:
                here, there = pl.ds(row, side), pl.ds(row, size - row)
                block = newton_one * half[here, there] + product(half_l, poly_r, row)
                gram[here, there] = block
                store(gram_l, gram_r, block, row)

    def turn(_, carry):
        advance(False)
        return carry

    lax.fori_loop(0, 4, turn, 0)
    advance(True)


def newton_chain(gram, rows, dtype):
    size, count = rows.shape[1], rows.shape[0]
    wide, tall = ((size, 3 * size), bf16), ((3 * size, size), bf16)
    shapes = [((size, size), f32), ((count, size), f32), ((size, size), f32)]
    shapes = shapes + [wide, tall, wide, tall, wide, ((count, 3 * size), bf16)]
    whole = pl.BlockSpec(memory_space=pltpu.VMEM)
    return pl.pallas_call(
        chain_kernel,
        out_shape=jax.ShapeDtypeStruct(rows.shape, dtype),
        in_specs=[whole] * 2,
        out_specs=whole,
        scratch_shapes=[pltpu.VMEM(*shape) for shape in shapes],
        compiler_params=pltpu.CompilerParams(vmem_limit_bytes=56 * 1024 * 1024),
        cost_estimate=pl.CostEstimate(
            flops=5 * (13 * size + 5 * count) * size * size,
            bytes_accessed=8 * gram.size,
            transcendentals=0,
        ),
    )(gram, rows)


def body(
    query_ids,
    passage_ids,
    passage_len,
    positives,
    domains,
    table,
    table_m,
    table_v,
    pos_table,
    pos_m,
    pos_v,
    vector,
    vector_m,
    vector_v,
    w_qkv,
    m_qkv,
    w_attn,
    m_attn,
    w_in,
    m_in,
    w_out,
    m_out,
    w_proj,
    m_proj,
):
    blocks = lax.axis_size("blk")
    narrow = lax.axis_size("narrow")
    devices = blocks * narrow
    both = ("blk", "narrow")
    myself = lax.axis_index("blk")
    shard_rows = table.shape[0]
    micro_count, _, query_len = query_ids.shape
    span = passage_ids.shape[2]
    length = query_len + span
    tokens = micro_count * length

    side = D // narrow
    vector_cols = vector.shape[1] // side
    small = jnp.concatenate(
        [
            low(pos_table).T,
            low(w_proj).T,
            low(vector).reshape(side, vector_cols),
            jnp.zeros((side, D - span - VDIM - vector_cols), bf16),
        ],
        axis=1,
    )


    def gather(shard):
        return lax.all_gather(shard, "narrow", axis=0, tiled=True)


    def gather(shard):
        return lax.all_gather(shard, "narrow", axis=0, tiled=True)

    first = gather(jnp.concatenate([small, low(w_attn).T], axis=1))
    small, attn_t = first[:, :D], first[:, D:]
    qkv_t = gather(low(w_qkv).T)
    in_t = gather(low(w_in).T)
    out_t = gather(low(w_out).T)
    pos = small[:, :span].T.astype(f32)
    proj_t = small[:, span : span + VDIM]
    gains = small[:, span + VDIM : span + VDIM + vector_cols].reshape(-1).astype(f32)
    bounds = [0, D, 2 * D, 3 * D, 4 * D, 5 * D, 6 * D, 7 * D, 7 * D + FF, 8 * D + FF, 9 * D + FF]
    bounds = bounds + [10 * D + FF]
    pieces = [gains[None, bounds[index] : bounds[index + 1]] for index in range(11)]
    qkv_bias = jnp.concatenate([pieces[2], jnp.zeros_like(pieces[2]), pieces[3]], axis=1)

    slots = round_up(SLOT_CAPS.get(shard_rows, tokens), 8)
    ids = jnp.concatenate([query_ids[:, 0], passage_ids[:, 0]], axis=1).reshape(tokens)
    owner = ids // shard_rows
    local_id = ids - owner * shard_rows
    is_owner = owner[:, None] == jnp.arange(devices, dtype=jnp.int32)[None]
    before = jnp.arange(tokens)[:, None] > jnp.arange(tokens)[None]
    earlier = dot_nn(before.astype(bf16), is_owner.astype(bf16))
    rank = jnp.sum(jnp.where(is_owner, earlier, 0.0), axis=1).astype(jnp.int32)
    place = owner * slots + rank
    picks = (place[:, None] == jnp.arange(devices * slots, dtype=jnp.int32)[None]).astype(bf16)
    picks_t = (jnp.arange(devices * slots, dtype=jnp.int32)[:, None] == place[None]).astype(bf16)
    picks = lax.optimization_barrier(picks)
    digits = jnp.stack([local_id // 32, local_id % 32], axis=1).astype(bf16)
    asked = dot_tn(digits, picks)
    asked = (asked[0] * 32.0 + asked[1]).astype(jnp.int32).reshape(devices, slots)
    wanted = lax.all_to_all(asked, both, 0, 0, tiled=True).reshape(devices * slots)
    chosen = (wanted[:, None] == jnp.arange(shard_rows, dtype=jnp.int32)[None]).astype(bf16)
    chosen_t = (jnp.arange(shard_rows, dtype=jnp.int32)[:, None] == wanted[None]).astype(bf16)
    chosen = lax.optimization_barrier(chosen)
    sent_rows = low(dot_nn(chosen, low(table))).reshape(devices, slots, D)
    got_rows = lax.all_to_all(sent_rows, both, 0, 0, tiled=True).reshape(devices * slots, D)
    token_rows = dot_nn(picks, got_rows)

    per = blocks // MATRICES
    turn_of = myself // per
    wide_rows = FF // devices

    def padded(rows):
        spare = wide_rows - rows.shape[-2]
        return jnp.pad(rows, ((0, 0),) * (rows.ndim - 2) + ((0, spare), (0, 0)))

    old = [padded(member.T.reshape(blocks, -1, D)) for member in (m_qkv, m_attn, m_in, m_out)]
    old = lax.dynamic_index_in_dim(jnp.stack(old), turn_of, 0, keepdims=False).reshape(-1, D)
    token_rows, old, picks_t, chosen_t = tie(token_rows, old, picks_t, chosen_t)

    lens = passage_len[:, 0]
    pos_rows = jnp.concatenate([pos[:query_len], pos] * micro_count, axis=0)
    x, x_hat, x_scale = norm_forward(token_rows + pos_rows, pieces[0], pieces[1])
    x_low = low(x)
    qkv = low(dot_nt(x_low, qkv_t) + qkv_bias)
    context, norms = attention_forward(lens, qkv, query_len, span)
    heads = round_up(HEADS, 8)
    norms = norms.reshape(micro_count, length, 128)[:, :, :heads].transpose(0, 2, 1)
    norms = jnp.concatenate([norms[:, :, query_len:], norms[:, :, :query_len]], axis=2)
    h, h_hat, h_scale = norm_forward(
        x + dot_nt(context, attn_t) + pieces[4], pieces[5], pieces[6]
    )
    h_low = low(h)
    wide = lax.optimization_barrier(dot_nt(h_low, in_t) + pieces[7])
    gelu_value, gelu_slope = gelu_parts(wide)
    f_low, gelu_slope = tie(low(gelu_value), low(gelu_slope))
    o, o_hat, o_scale = norm_forward(h + dot_nn(f_low, out_t) + pieces[8], pieces[9], pieces[10])
    o_low = low(o)
    e = dot_nn(o_low, proj_t)
    e_scale = lax.rsqrt(jnp.sum(e * e, axis=-1, keepdims=True) + 1e-06)
    vecs = low(e * e_scale)

    labels = domains[:, 0]
    targets = positives[:, 0]
    spots = jnp.arange(blocks, dtype=jnp.int32)
    chosen_label = jnp.sum(
        jnp.where(targets[:, :, None] == spots[None, None], labels[:, None, :], 0), axis=-1
    )

    def spread(mask):
        mask = mask.astype(f32).transpose(1, 0, 2).reshape(blocks, micro_count * blocks, 1)
        return jnp.broadcast_to(mask, (blocks, micro_count * blocks, 128))

    allowed = spread(labels[:, :, None] == chosen_label[:, None, :])
    hits = spread(targets[:, None, :] == spots[None, :, None])
    vecs, allowed, hits = tie(vecs, allowed, hits)
    by_micro = vecs.reshape(micro_count, length, VDIM)
    cycle = by_micro[:, :query_len].reshape(micro_count * query_len, VDIM)
    cycle = share_all(cycle, "blk", blocks).reshape(blocks, micro_count * query_len, VDIM)
    share, scores = score_forward(lens, cycle, vecs, query_len, span)
    every = share_all(scores.reshape(micro_count * blocks, 128), "blk", blocks)
    every = every.reshape(blocks, micro_count * blocks, 128)
    loss_part, d_passage, d_cycle = score_backward(
        myself, every, allowed, hits, share, cycle, vecs, query_len, span
    )
    loss_part = loss_part[0, 0]
    d_query = jnp.sum(lax.all_to_all(d_cycle, "blk", 0, 0, tiled=True), axis=0)
    d_query = d_query.reshape(micro_count, query_len, VDIM)
    d_vecs = jnp.concatenate([d_query, d_passage], axis=1).reshape(tokens, VDIM)

    def reduction(pieces, wire):
        return Reduction(pieces[1::2], pieces[0::2], narrow, blocks, wire)

    def column_sum(values):
        return jnp.sum(values, axis=0)

    d_vecs = low(d_vecs).astype(f32)
    inner = jnp.sum(e * d_vecs, axis=-1, keepdims=True)
    d_e = low(e_scale * d_vecs - e * (e_scale * e_scale * e_scale * inner))
    g_proj = dot_tn(o_low, d_e)
    d_o = low(dot_nt(d_e, proj_t)).astype(f32)
    g_gain_o, g_shift_o = column_sum(d_o * o_hat), column_sum(d_o)
    d_sum_o = norm_backward(d_o, o_hat, o_scale, pieces[9])
    g_bias_out = column_sum(d_sum_o)
    d_y = low(d_sum_o)
    place = lax.axis_index("narrow")
    low_bit = place & 1
    g_out = dot_tn(f_low, d_y).reshape(narrow // 2, 2, -1, D)
    out_sent = lax.dynamic_index_in_dim(g_out, 1 - low_bit, 1, keepdims=False)
    d_y, out_sent, g_out = tie(d_y, out_sent, g_out)
    out_got = swap(out_sent, "narrow", narrow, 1)
    d_f = low(dot_nt(d_y, out_t)).astype(f32)
    d_wide = d_f * gelu_slope.astype(f32)
    g_bias_in = column_sum(d_wide)
    d_wide = low(d_wide)
    d_wide, out_got = tie(d_wide, out_got)
    g_out = lax.dynamic_index_in_dim(g_out, low_bit, 1, keepdims=False) + out_got
    g_out = low(g_out.reshape(-1, D))
    d_wide, g_out = tie(d_wide, g_out)
    if narrow > 2:
        groups = [list(range(bit, narrow, 2)) for bit in range(2)]
        g_out = lax.psum_scatter(
            g_out, "narrow", scatter_dimension=0, axis_index_groups=groups, tiled=True
        )
    sum_in = reduction(relative(dot_tn(d_wide, h_low), narrow), bf16)
    d_wide, sum_in.sent = tie(d_wide, sum_in.sent)
    sum_in.across_core()
    d_wide, sum_in.kept = tie(d_wide, sum_in.kept)
    sum_in.prepare()
    d_wide, sum_in.outgoing, sum_in.kept = tie(d_wide, sum_in.outgoing, sum_in.kept)
    sum_in.send()
    d_h = d_sum_o + low(dot_nn(d_wide, in_t)).astype(f32)
    g_gain_h, g_shift_h = column_sum(d_h * h_hat), column_sum(d_h)
    d_sum_h = norm_backward(d_h, h_hat, h_scale, pieces[5])
    g_bias_attn = column_sum(d_sum_h)
    d_a = low(d_sum_h)
    sum_attn = reduction(relative(dot_tn(d_a, context), narrow), bf16)
    d_a, sum_attn.sent, g_out = tie(d_a, sum_attn.sent, g_out)
    g_out = lax.psum_scatter(g_out.astype(f32), "blk", scatter_dimension=0, tiled=True)
    sum_attn.across_core()
    d_context = low(dot_nn(d_a, attn_t))
    d_context, sum_attn.got = tie(d_context, sum_attn.got)
    sum_attn.across_narrow()
    head_of = jnp.arange(D)[None] // HDIM == jnp.arange(heads)[:, None]
    inner = lax.dot_general(
        head_of.astype(f32),
        d_context.astype(f32) * context.astype(f32),
        (((1,), (1,)), ((), ())),
        precision=lax.Precision.HIGH,
        preferred_element_type=f32,
    )
    inner = inner.reshape(heads, micro_count, length).transpose(1, 0, 2)
    inner = jnp.concatenate([inner[:, :, query_len:], inner[:, :, :query_len]], axis=2)
    d_qkv = attention_backward(lens, qkv, d_context, norms, inner, query_len, span)
    d_qkv, sum_in.got, sum_attn.got = tie(d_qkv, sum_in.got, sum_attn.got)
    g_in = sum_in.total()
    d_qkv, g_in = tie(d_qkv, g_in)
    g_in = lax.psum_scatter(g_in, "blk", scatter_dimension=0, tiled=True)
    d_x = d_sum_h + low(dot_nn(d_qkv, qkv_t)).astype(f32)
    d_rows = norm_backward(d_x, x_hat, x_scale, pieces[0])

    back_rows = low(dot_nn(picks_t, low(d_rows))).reshape(devices, slots, D)
    back_rows, d_rows, d_x, d_qkv, g_proj = tie(back_rows, d_rows, d_x, d_qkv, g_proj)
    back_rows = lax.all_to_all(back_rows, both, 0, 0, tiled=True).reshape(devices * slots, D)
    sum_qkv = reduction(relative(dot_tn(d_qkv, x_low), narrow), bf16)
    d_qkv, d_rows, d_x, sum_qkv.sent = tie(d_qkv, d_rows, d_x, sum_qkv.sent)
    sum_qkv.across_core()
    sum_qkv.across_narrow()
    early = (g_bias_attn, g_gain_h, g_shift_h, g_bias_in, g_bias_out, g_gain_o, g_shift_o)
    tail = late_sums(d_rows, d_x, x_hat, d_qkv, g_proj, early, query_len, span, micro_count)
    sum_tail = reduction(relative(tail, narrow), f32)
    sum_tail.across_core()
    sum_tail.across_narrow()
    tail = sum_tail.total()
    spare_high = lax.optimization_barrier(low(tail[:, span:]))
    tail = [low(tail[:, :span]), spare_high, low(tail[:, span:] - spare_high.astype(f32))]
    tail = jnp.concatenate(tail, axis=1).reshape(blocks, -1)
    tail_size = tail.shape[1]
    tail = jnp.pad(tail, ((0, 0), (0, round_up(tail_size, 16 * D) - tail_size)))
    merged = [low(member.total()).reshape(blocks, -1, D) for member in (sum_qkv, sum_attn)]
    merged = jnp.concatenate(merged + [tail.reshape(blocks, -1, D)], axis=1)
    merged, back_rows = tie(merged, back_rows)
    merged = lax.all_to_all(merged, "blk", 0, 0, tiled=True)
    table_grad = dot_nn(chosen_t, back_rows)
    table_square = jnp.sum(table_grad * table_grad)
    merged = jnp.sum(merged.astype(f32), axis=0)
    attn_rows = D // devices
    qkv_rows = 3 * attn_rows
    g_qkv, g_attn = merged[:qkv_rows], merged[qkv_rows : qkv_rows + attn_rows]
    g_tail = merged[qkv_rows + attn_rows :].reshape(-1)[:tail_size].reshape(attn_rows, -1)
    spare = g_tail[:, span : span + 128 + VDIM] + g_tail[:, span + 128 + VDIM :]
    g_tail = jnp.concatenate([g_tail[:, :span], spare], axis=1)
    g_qkv, g_attn, g_out, g_in, g_tail, table_square = tie(
        g_qkv, g_attn, g_out, g_in, g_tail, table_square
    )

    sends = [padded(low(member)) for member in (g_qkv, g_attn, g_in, g_out)]
    sends = jnp.repeat(jnp.stack(sends), per, axis=0)
    taken = lax.all_to_all(sends, "blk", 0, 0, tiled=True)

    def square_sum(values):
        values = values.astype(f32)
        return jnp.sum(values * values)

    local_square = (
        table_square
        + square_sum(g_out)
        + square_sum(g_in)
        + square_sum(g_qkv)
        + square_sum(g_attn)
        + square_sum(g_tail)
    )
    lane = lax.broadcasted_iota(jnp.int32, (8, 128), 1)
    pair = jnp.where(lane == 0, local_square, jnp.where(lane == 1, loss_part, 0.0))
    sums = sum_everywhere(pair, (("narrow", narrow), ("blk", blocks)))
    loss = sums[0, 1]
    grad_norm = jnp.sqrt(sums[0, 0])
    factor = jnp.minimum(1.0, clip_limit / (grad_norm + 1e-06))

    packed = [low(member) for member in (g_qkv, g_attn, g_in, g_out, g_tail)]
    complete = lax.all_gather(jnp.concatenate(packed, axis=0), "blk", axis=0, tiled=False)
    moment, gram = packed_gram(factor, old, taken.reshape(-1, D))
    gram = sum_group(gram, narrow, 1, blocks)
    half = moment.shape[0] // per
    moment = lax.dynamic_slice_in_dim(moment, myself % per * half, half, axis=0)
    ortho = newton_chain(gram, moment, bf16)
    ortho, complete = tie(ortho, complete)
    ortho = lax.all_gather(ortho, "blk", axis=0, tiled=False)
    ortho = ortho.reshape(MATRICES, blocks, wide_rows, D)
    matrix_rows = (qkv_rows, attn_rows, wide_rows, wide_rows)

    def turned(rows):
        return rows.reshape(-1, D).T.astype(f32)

    grads, first = [], 0
    for rows in matrix_rows:
        grads.append(turned(complete[:, first : first + rows]))
        first += rows
    tail_all = complete[:, first:].reshape(side, -1)
    grad_pos = tail_all[:, :span].T.astype(f32)
    grad_proj = tail_all[:, span + 128 :].T.astype(f32)
    grad_vector = tail_all[:, span : span + 128].T
    grad_bias = grad_vector[4:5].astype(f32)
    place = lax.axis_index("narrow")
    whole_vector = jnp.zeros((narrow,) + grad_vector.shape, bf16)
    for offset, piece in enumerate(gather_relative(grad_vector, narrow)):
        whole_vector = lax.dynamic_update_index_in_dim(whole_vector, piece, place ^ offset, 0)
    whole_vector = whole_vector.transpose(1, 0, 2)[:vector_cols].reshape(1, -1).astype(f32)
    grad_vector = lax.dynamic_slice_in_dim(
        whole_vector, place * vector.shape[1], vector.shape[1], axis=1
    )
    proj_rows, gram_proj = packed_gram(factor, m_proj.T, grad_proj.T)
    ortho_proj = newton_chain(sum_group(gram_proj, narrow, 1, blocks), proj_rows, f32)
    table_new, table_m_new, table_v_new = adam_step(
        table, table_m, table_v, factor * table_grad, adam_rate
    )
    pos_new, pos_m_new, pos_v_new = adam_step(
        pos_table, pos_m, pos_v, factor * grad_pos, adam_rate
    )
    vector_new, vector_m_new, vector_v_new = adam_step(
        vector, vector_m, vector_v, factor * grad_vector, vector_rate
    )
    olds = (m_qkv, m_attn, m_in, m_out, m_proj)
    grads = grads + [grad_proj]
    moments = [muon_moment * before + factor * grad for before, grad in zip(olds, grads)]
    masters = (w_qkv, w_attn, w_proj)
    orthos = (turned(ortho[0, :, :qkv_rows]), turned(ortho[1, :, :attn_rows]), ortho_proj.T)
    updated = []
    for weight, ortho_part, rate in zip(masters, orthos, (muon_rate, attn_rate, muon_rate)):
        long_side = max(weight.shape[0], weight.shape[1] * narrow)
        updated.append(weight - rate * (0.2 * long_side**0.5 * ortho_part + weight_decay * weight))
    wide_orthos = [ortho[index].reshape(-1, D) for index in (2, 3)]
    in_new, out_new = update_wide((w_in, w_out), wide_orthos, muon_rate, 0.2 * FF**0.5)
    updated = [updated[0], updated[1], in_new, out_new, updated[2]]
    return (
        loss,
        grad_norm,
        table_new,
        table_m_new,
        table_v_new,
        pos_new,
        pos_m_new,
        pos_v_new,
        vector_new,
        vector_m_new,
        vector_v_new,
        updated[0],
        moments[0],
        updated[1],
        moments[1],
        updated[2],
        moments[2],
        updated[3],
        moments[3],
        updated[4],
        moments[4],
        factor * grad_bias,
    )


def solution(mesh):
    ids = P(None, ("blk", "narrow"), None)
    rows = P(("blk", "narrow"), None)
    cols = P(None, "narrow")
    group = P(None, "narrow", None)
    in_specs = (ids, ids, P(None, ("blk", "narrow")), group, group) + (rows,) * 3 + (cols,) * 16
    out_specs = (P(), P()) + (rows,) * 3 + (cols,) * 17
    return jax.shard_map(body, mesh=mesh, in_specs=in_specs, out_specs=out_specs, check_vma=False)
```
